256 devices in a mesh: batch: 32 (over x, z_lo, core), field: 8 (over y, z_hi).
Axes of the slice: x: 4, y: 4, z: 8 (z_hi: 2, z_lo: 4; z = z_hi * 4 + z_lo), core: 2. Of those that a mesh axis runs over, the one named last changes fastest.
Arguments:
- emb_tables: bfloat16 [256, 8192, 128], P(('field', 'batch')), may hold values from -3 to 3
- bag_ids: int32 [256, 6144, 8], P(('field', 'batch')), may hold values from 0 to 8191
- bag_lengths: int32 [256, 6144], P(('field', 'batch')), may hold values from 1 to 8
- table_widths: int32 [256], P(('field', 'batch')), may hold values from 16 to 128
- projection: bfloat16 [256, 128, 64], P('field'), may hold values from -0.5 to 0.5
- cross_u: bfloat16 [2, 512, 16384], P(None, 'batch', 'field'), may hold values from -0.25 to 0.25
- cross_v: bfloat16 [2, 512, 16384], P(None, 'batch', 'field'), may hold values from -0.046875 to 0.046875
- cross_bias: float32 [2, 16384], P(None, 'field'), may hold values from -3 to 3
- cotangent: bfloat16 [6144, 16384], P('batch', 'field'), may hold values from -6 to 6
Outputs:
- crossed: bfloat16 [6144, 16384], P('batch', 'field')
- grad_u: float32 [2, 512, 16384], P(None, 'batch', 'field')
- grad_v: float32 [2, 512, 16384], P(None, 'batch', 'field')
- grad_bias: float32 [2, 16384], P(None, ('field', 'batch'))
- grad_projection: float32 [256, 128, 64], P(('field', 'batch'))
- grad_pooled: bfloat16 [256, 6144, 128], P(('field', 'batch'))
The draws below stay inside these ranges and needn't reach their ends.
All inputs are finite; a program needn't handle non-finite values.
Results may differ from the reference program's by a relative error of at most 0.039.
Values may be sent and summed in bfloat16 or wider, within the bound.
No kernel may reach another device: no remote copies, remote signals or barrier semaphores. Data moves between devices by JAX's collectives and lax.ppermute only.
A program may use at most 128 MiB of HBM per device.

```python
import math
import jax
import jax.numpy as jnp
import numpy as np
from jax import lax

B_DEV = 192
ROWS = 8192
EMAX = 128
PW = 64
BAG = 8
R = 512
LAYERS = 2
TABLES = 256
TOKENS = 6144
D = 16384
N_BATCH = 32


def place_ends(values, key, least, largest):
    dims = values.shape
    place = [jax.random.randint(jax.random.fold_in(key, axis), (), 0, dims[axis]) for axis in range(len(dims))]
    values = values.at[tuple(place)].set(least)
    longest = dims.index(max(dims))
    place[longest] = (place[longest] + 1) % dims[longest]
    return values.at[tuple(place)].set(largest)


def level_of(rng, shape, cuts, least, top_value):
    factor_of, own = 1.0, jax.random.fold_in(rng, 6)
    for position, parts in cuts:
        draws = jnp.exp(jax.random.uniform(jax.random.fold_in(own, position), (parts,), jnp.float32, least / len(cuts), top_value / len(cuts)))
        factor_of = factor_of * jnp.repeat(draws, shape[position] // parts).reshape([-1 if axis == position else 1 for axis in range(len(shape))])
    return factor_of


def rank_table(amount, skew):
    weights = [(1 << 20) // math.isqrt(rank ** skew) + 1 for rank in range(1, amount + 1)]
    spread = 1 + sum(weights) // (1 << 30)
    return np.cumsum(np.array([max(1, weight // spread) for weight in weights]))


def skewed_ids(rng, extent, amount, slope):
    listing = rank_table(amount, slope)
    lot = jax.random.randint(jax.random.fold_in(rng, 1), extent, 0, int(listing[amount - 1]))
    rank = jnp.searchsorted(jnp.asarray(listing, jnp.int32), lot, side="right")
    return jax.random.permutation(jax.random.fold_in(rng, 2), amount)[rank].astype(jnp.int32)


def noise(stream_key, extent, width, most, cuts=(), kind=jnp.bfloat16):
    result = width * jax.random.normal(stream_key, extent, jnp.float32)
    if cuts:
        result = result * level_of(stream_key, extent, cuts, -0.22, 0.18)
    return jnp.clip(result, -most, most).astype(kind)


def setup_inputs(seed: int = 0) -> dict:
    seeds = jax.random.split(jax.random.key(seed), 10)
    return {
        "emb_tables": noise(seeds[0], (TABLES, ROWS, EMAX), 0.5, 3.0, ((0, 256),)),
        "bag_ids": place_ends(skewed_ids(seeds[1], (TABLES, TOKENS, BAG), ROWS, 2), jax.random.fold_in(seeds[1], 3), 0, ROWS - 1).astype(jnp.int32),
        "bag_lengths": place_ends(jax.random.randint(seeds[2], (TABLES, TOKENS), 1, BAG + 1), jax.random.fold_in(seeds[2], 1), 1, BAG).astype(jnp.int32),
        "table_widths": place_ends(jax.random.randint(seeds[3], (TABLES,), 16, EMAX + 1), jax.random.fold_in(seeds[3], 1), 16, EMAX).astype(jnp.int32),
        "projection": noise(seeds[4], (TABLES, EMAX, PW), EMAX ** -0.5, 0.5, ((0, 8),)),
        "cross_u": noise(seeds[5], (LAYERS, R, D), R ** -0.5, 0.25, ((1, 32), (2, 8))),
        "cross_v": noise(seeds[6], (LAYERS, R, D), D ** -0.5, 0.046875, ((1, 32), (2, 8))),
        "cross_bias": noise(seeds[7], (LAYERS, D), 0.5, 3.0, ((1, 8),), jnp.float32),
        "cotangent": noise(seeds[8], (TOKENS, D), 1.0, 6.0, ((0, 32), (1, 8))),
    }


def wire_round(value):
    return lax.optimization_barrier(value.astype(jnp.bfloat16)).astype(jnp.float32)


def pool_table(emb_table, block_ids, block_lengths):
    looked_up = jnp.take(emb_table, block_ids, axis=0).astype(jnp.float32)
    places = jnp.arange(BAG, dtype=jnp.int32)
    active = places[None, :] < block_lengths[:, None]
    return jnp.sum(jnp.where(active[:, :, None], looked_up, 0.0), axis=1)


def reference(emb_tables, bag_ids, bag_lengths, table_widths, projection, cross_u, cross_v, cross_bias, cotangent):
    columns = jnp.arange(EMAX, dtype=jnp.int32)
    within = columns[None, None, :] < table_widths[:, None, None]
    proj_wide = projection.astype(jnp.float32)
    ids_blocks = jnp.transpose(bag_ids.reshape(TABLES, N_BATCH, B_DEV, BAG), (1, 0, 2, 3))
    length_blocks = jnp.transpose(bag_lengths.reshape(TABLES, N_BATCH, B_DEV), (1, 0, 2))
    cot_blocks = cotangent.reshape(N_BATCH, B_DEV, D)

    def one_block(running, inputs):
        total_u, total_v, total_bias, total_proj = running
        block_ids, block_lengths, block_cot = inputs
        pooled_sum = jax.vmap(pool_table)(emb_tables, block_ids, block_lengths)
        pooled = jnp.where(within, pooled_sum, 0.0).astype(jnp.bfloat16)
        pooled_wide = pooled.astype(jnp.float32)
        projected = jnp.einsum("tse,tep->tsp", pooled_wide, proj_wide).astype(jnp.bfloat16)
        initial = jnp.transpose(projected, (1, 0, 2)).reshape(B_DEV, D)
        initial_wide = initial.astype(jnp.float32)
        current = initial
        layer_inputs = []
        rank_lows = []
        hiddens = []
        for layer_index in range(LAYERS):
            rank_sum = jnp.dot(current, cross_v[layer_index].T, preferred_element_type=jnp.float32)
            rank_low = rank_sum.astype(jnp.bfloat16)
            hidden = jnp.dot(rank_low, cross_u[layer_index], preferred_element_type=jnp.float32) + cross_bias[layer_index][None, :]
            layer_inputs.append(current)
            rank_lows.append(rank_low)
            hiddens.append(hidden)
            current = (initial_wide * hidden + current.astype(jnp.float32)).astype(jnp.bfloat16)
        upstream = block_cot.astype(jnp.float32)
        base_grad = jnp.zeros_like(upstream)
        for layer_index in reversed(range(LAYERS)):
            hidden_grad = (upstream * initial_wide).astype(jnp.bfloat16)
            base_grad = base_grad + upstream * hiddens[layer_index]
            u_term = jnp.dot(rank_lows[layer_index].T, hidden_grad, preferred_element_type=jnp.float32)
            bias_term = jnp.sum(hidden_grad.astype(jnp.float32), axis=0)
            rank_grad = jnp.dot(hidden_grad, cross_u[layer_index].T, preferred_element_type=jnp.float32).astype(jnp.bfloat16)
            v_term = jnp.dot(rank_grad.T, layer_inputs[layer_index], preferred_element_type=jnp.float32)
            upstream = upstream + jnp.dot(rank_grad, cross_v[layer_index], preferred_element_type=jnp.float32)
            total_u = total_u.at[layer_index].add(wire_round(u_term))
            total_v = total_v.at[layer_index].add(wire_round(v_term))
            total_bias = total_bias.at[layer_index].add(wire_round(bias_term))
        input_grad = (upstream + base_grad).astype(jnp.bfloat16)
        table_grad = jnp.transpose(input_grad.reshape(B_DEV, TABLES, PW), (1, 0, 2)).astype(jnp.float32)
        pooled_grad = jnp.where(within, jnp.einsum("tsp,tep->tse", table_grad, proj_wide), 0.0).astype(jnp.bfloat16)
        total_proj = total_proj + jnp.einsum("tse,tsp->tep", pooled_wide, table_grad)
        return (total_u, total_v, total_bias, total_proj), (current, pooled_grad)

    start = (jnp.zeros((LAYERS, R, D), jnp.float32), jnp.zeros((LAYERS, R, D), jnp.float32),
             jnp.zeros((LAYERS, D), jnp.float32), jnp.zeros((TABLES, EMAX, PW), jnp.float32))
    finals, outputs = lax.scan(one_block, start, (ids_blocks, length_blocks, cot_blocks))
    crossed_blocks, grad_blocks = outputs
    crossed = crossed_blocks.reshape(TOKENS, D)
    grad_pooled = jnp.transpose(grad_blocks, (1, 0, 2, 3)).reshape(TABLES, TOKENS, EMAX)
    return (crossed, finals[0], finals[1], finals[2], finals[3], grad_pooled)
```

```python
import functools

import jax
import jax.numpy as jnp
from jax import lax
from jax.experimental import pallas as pl
from jax.experimental.pallas import tpu as pltpu
from jax.sharding import PartitionSpec as P

BF16 = jnp.bfloat16
F32 = jnp.float32
MIB = 2**20

X_SIZE, Z_SIZE, CORES = 4, 4, 2
Y_SIZE, HALVES = 4, 2

ROWS, EMB, PROJ, BAG = 8192, 128, 64, 8
SAMPLES, FEATURES, RANK = 192, 2048, 512
FIELD_TABLES = 32
HALF = SAMPLES // 2
SHARE = RANK // FIELD_TABLES
TOKENS = SAMPLES * FIELD_TABLES
BACK_ROWS = HALF + 16
FEATURE_BLOCK = 256
POOL_CHUNK = 768
POOL_UNROLL = 32
QUARTER = 2 * SAMPLES // Y_SIZE

AT_BATCH, AT_X, AT_Z, AT_CORE, AT_Y, AT_WIDTH = range(6)
U0, U1, V0, V1 = range(4)


def params():
    return pltpu.CompilerParams(vmem_limit_bytes=48 * MIB)


def cost(flops, moved):
    return pl.CostEstimate(flops=flops, bytes_accessed=moved, transcendentals=0)


def dot(left, right, left_dim, right_dim):
    return lax.dot_general(
        left, right, (((left_dim,), (right_dim,)), ((), ())), preferred_element_type=F32
    )


def masked_projection(proj_ref, width):
    columns = lax.broadcasted_iota(jnp.int32, (PROJ, EMB), 1)
    return jnp.where(columns < width, proj_ref[0].astype(F32), 0.0).astype(BF16)


def pool_kernel(at, ids, table, proj, pooled, sent, wide_table, summed):
    @pl.when(pl.program_id(0) == 0)
    def _():
        within = lax.broadcasted_iota(jnp.int32, (256, EMB), 1) < at[AT_WIDTH]

        @pl.loop(0, ROWS // 256)
        def _(part):
            rows = pl.ds(pl.multiple_of(part * 256, 256), 256)
            wide_table[rows, :] = jnp.where(within, table[rows, :].astype(F32), 0.0)

        wide_table[ROWS : ROWS + 8, :] = jnp.zeros((8, EMB), F32)

    groups = 128 // POOL_UNROLL

    @pl.loop(0, POOL_CHUNK // POOL_UNROLL)
    def _(group):
        first = group * POOL_UNROLL
        base = (group // groups) * (128 * BAG) + (group % groups) * POOL_UNROLL
        for step in range(POOL_UNROLL):
            rows = [wide_table[pl.ds(ids[base + (place * 128 + step)], 1), :] for place in range(BAG)]
            summed[pl.ds(first + step, 1), :] = (
                (rows[0] + rows[1]) + (rows[2] + rows[3])
            ) + ((rows[4] + rows[5]) + (rows[6] + rows[7]))

    low = summed[...].astype(BF16)
    pooled[...] = low
    factor = proj[0]
    none = jnp.zeros_like(factor)
    both = jnp.concatenate(
        [jnp.concatenate([factor, none], axis=1), jnp.concatenate([none, factor], axis=1)], axis=0
    )
    for block in range(POOL_CHUNK // SAMPLES):
        start = block * SAMPLES
        pair = jnp.concatenate(
            [low[start : start + HALF], low[start + HALF : start + SAMPLES]], axis=1
        )
        sent[block] = dot(pair, both, 1, 1).astype(BF16)


def pool(at, ids, table, proj):
    blocks = POOL_CHUNK // SAMPLES
    return pl.pallas_call(
        pool_kernel,
        grid_spec=pltpu.PrefetchScalarGridSpec(
            num_scalar_prefetch=1,
            grid=(TOKENS // POOL_CHUNK,),
            in_specs=[
                pl.BlockSpec((POOL_CHUNK * BAG,), lambda i, at: (i,), memory_space=pltpu.SMEM),
                pl.BlockSpec((ROWS, EMB), lambda i, at: (0, 0)),
                pl.BlockSpec((1, PROJ, EMB), lambda i, at: (at[AT_BATCH], 0, 0)),
            ],
            out_specs=[
                pl.BlockSpec((POOL_CHUNK, EMB), lambda i, at: (i, 0)),
                pl.BlockSpec((blocks, HALF, EMB), lambda i, at: (i, 0, 0)),
            ],
            scratch_shapes=[pltpu.VMEM((ROWS + 8, EMB), F32), pltpu.VMEM((POOL_CHUNK, EMB), F32)],
        ),
        out_shape=[
            jax.ShapeDtypeStruct((TOKENS, EMB), BF16),
            jax.ShapeDtypeStruct((FIELD_TABLES, HALF, EMB), BF16),
        ],
        compiler_params=params(),
        cost_estimate=cost(2 * 10**9, 100 * MIB),
    )(at, ids, table, proj)


def write_quarters(at, total, parts):
    for shift, part in enumerate(parts):
        place = lax.rem(at[AT_Y] + shift, Y_SIZE)
        part[...] = total[pl.ds(pl.multiple_of(place * QUARTER, QUARTER), QUARTER), :].astype(BF16)


def read_quarters(at, parts, whole):
    for shift, part in enumerate(parts):
        place = lax.rem(at[AT_Y] + Y_SIZE - shift, Y_SIZE)
        whole[pl.ds(pl.multiple_of(place * QUARTER, QUARTER), QUARTER), :] = part[...]


def weight(ref):
    return ref[...].reshape(RANK, FEATURE_BLOCK)


def first_kernel(at, recv, cot, v0, u1, x0_out, hg_out, bias_out, *rest):
    parts, total = rest[:4], rest[4]
    step = pl.program_id(0)
    columns = []
    for pair in range(FEATURE_BLOCK // EMB):
        left, right = recv[2 * pair], recv[2 * pair + 1]
        top = jnp.concatenate([left[:, :PROJ], right[:, :PROJ]], axis=1)
        bottom = jnp.concatenate([left[:, PROJ:], right[:, PROJ:]], axis=1)
        columns.append(jnp.concatenate([top, bottom], axis=0))
    x0 = jnp.concatenate(columns, axis=1)
    hg = (cot[...].astype(F32) * x0.astype(F32)).astype(BF16)
    x0_out[...] = x0
    hg_out[...] = hg
    bias_out[...] = jnp.sum(hg.astype(F32), axis=0, keepdims=True)
    rank = dot(x0, weight(v0), 1, 1)
    rank_grad = dot(hg, weight(u1), 1, 1)

    @pl.when(step == 0)
    def _():
        total[:SAMPLES, :] = rank
        total[SAMPLES:, :] = rank_grad

    @pl.when(step > 0)
    def _():
        total[:SAMPLES, :] += rank
        total[SAMPLES:, :] += rank_grad

    @pl.when(step == pl.num_programs(0) - 1)
    def _():
        write_quarters(at, total, parts)


def feature_spec(rows):
    return pl.BlockSpec((rows, FEATURE_BLOCK), lambda j, at: (0, j))


def weight_spec(which):
    return pl.BlockSpec(
        (FIELD_TABLES, 1, SHARE, FEATURE_BLOCK), lambda j, at: (0, which, 0, j)
    )


def whole_spec(*shape):
    return pl.BlockSpec(shape, lambda j, at: (0,) * len(shape))


QUARTER_SPECS = [whole_spec(QUARTER, RANK) for _ in range(Y_SIZE)]
QUARTER_SHAPES = [jax.ShapeDtypeStruct((QUARTER, RANK), BF16) for _ in range(Y_SIZE)]
FEATURE_STEPS = FEATURES // FEATURE_BLOCK
TABLES_STEP = FEATURE_BLOCK // PROJ


def first(at, recv, cot, weights):
    return pl.pallas_call(
        first_kernel,
        grid_spec=pltpu.PrefetchScalarGridSpec(
            num_scalar_prefetch=1,
            grid=(FEATURE_STEPS,),
            in_specs=[
                pl.BlockSpec((TABLES_STEP, HALF, EMB), lambda j, at: (j, 0, 0)),
                feature_spec(SAMPLES),
                weight_spec(V0),
                weight_spec(U1),
            ],
            out_specs=[feature_spec(SAMPLES), feature_spec(SAMPLES), feature_spec(1)] + QUARTER_SPECS,
            scratch_shapes=[pltpu.VMEM((2 * SAMPLES, RANK), F32)],
        ),
        out_shape=[
            jax.ShapeDtypeStruct((SAMPLES, FEATURES), BF16),
            jax.ShapeDtypeStruct((SAMPLES, FEATURES), BF16),
            jax.ShapeDtypeStruct((1, FEATURES), F32),
        ]
        + QUARTER_SHAPES,
        compiler_params=params(),
        cost_estimate=cost(10**9, 8 * MIB),
    )(at, recv, cot, weights, weights)


def second_kernel(at, q0, q1, q2, q3, x0_ref, cot, u0_ref, v1_ref, bias, x1_out, hg_out, base_out, bias_out, *rest):
    parts, total, ranks = rest[:4], rest[4], rest[5]
    step = pl.program_id(0)

    @pl.when(step == 0)
    def _():
        read_quarters(at, (q0, q1, q2, q3), ranks)

    u0, v1 = weight(u0_ref), weight(v1_ref)
    x0 = x0_ref[...].astype(F32)
    hidden = dot(ranks[:SAMPLES, :], u0, 1, 0) + bias[0:1, :]
    upstream = cot[...].astype(F32) + dot(ranks[SAMPLES:, :], v1, 1, 0)
    x1 = (x0 * hidden + x0).astype(BF16)
    hg = (upstream * x0).astype(BF16)
    x1_out[...] = x1
    hg_out[...] = hg
    base_out[...] = upstream + upstream * hidden
    bias_out[...] = jnp.sum(hg.astype(F32), axis=0, keepdims=True)
    rank = dot(x1, v1, 1, 1)
    rank_grad = dot(hg, u0, 1, 1)

    @pl.when(step == 0)
    def _():
        total[:SAMPLES, :] = rank
        total[SAMPLES:, :] = rank_grad

    @pl.when(step > 0)
    def _():
        total[:SAMPLES, :] += rank
        total[SAMPLES:, :] += rank_grad

    @pl.when(step == pl.num_programs(0) - 1)
    def _():
        write_quarters(at, total, parts)


def second(at, quarters, x0, cot, weights, bias):
    return pl.pallas_call(
        second_kernel,
        grid_spec=pltpu.PrefetchScalarGridSpec(
            num_scalar_prefetch=1,
            grid=(FEATURE_STEPS,),
            in_specs=QUARTER_SPECS
            + [feature_spec(SAMPLES), feature_spec(SAMPLES), weight_spec(U0), weight_spec(V1), feature_spec(2)],
            out_specs=[feature_spec(SAMPLES), feature_spec(SAMPLES), feature_spec(SAMPLES), feature_spec(1)]
            + QUARTER_SPECS,
            scratch_shapes=[pltpu.VMEM((2 * SAMPLES, RANK), F32), pltpu.VMEM((2 * SAMPLES, RANK), BF16)],
        ),
        out_shape=[
            jax.ShapeDtypeStruct((SAMPLES, FEATURES), BF16),
            jax.ShapeDtypeStruct((SAMPLES, FEATURES), BF16),
            jax.ShapeDtypeStruct((SAMPLES, FEATURES), F32),
            jax.ShapeDtypeStruct((1, FEATURES), F32),
        ]
        + QUARTER_SHAPES,
        compiler_params=params(),
        cost_estimate=cost(2 * 10**9, 10 * MIB),
    )(at, *quarters, x0, cot, weights, weights, bias)


def third_kernel(at, q0, q1, q2, q3, x0_ref, x1_ref, cot, base, u1_ref, v0_ref, bias, sum0, sum1, crossed, back, ranks):
    @pl.when(pl.program_id(0) == 0)
    def _():
        read_quarters(at, (q0, q1, q2, q3), ranks)

    hidden = dot(ranks[:SAMPLES, :], weight(u1_ref), 1, 0) + bias[1:2, :]
    crossed[...] = (x0_ref[...].astype(F32) * hidden + x1_ref[...].astype(F32)).astype(BF16)
    grad = base[...] + dot(ranks[SAMPLES:, :], weight(v0_ref), 1, 0) + cot[...].astype(F32) * hidden
    grad = grad.astype(BF16)
    for table in range(TABLES_STEP):
        columns = slice(table * PROJ, (table + 1) * PROJ)
        back[table, :HALF, :] = jnp.concatenate([grad[:HALF, columns], grad[HALF:, columns]], axis=1)
        row = jnp.concatenate([sum0[:, columns], sum1[:, columns]], axis=1)
        first_row = lax.broadcasted_iota(jnp.int32, (16, EMB), 0) == 0
        back[table, HALF:, :] = jnp.where(first_row, row, 0.0).astype(BF16)


def third(at, quarters, x0, x1, cot, base, weights, bias, sum0, sum1):
    return pl.pallas_call(
        third_kernel,
        grid_spec=pltpu.PrefetchScalarGridSpec(
            num_scalar_prefetch=1,
            grid=(FEATURE_STEPS,),
            in_specs=QUARTER_SPECS
            + [feature_spec(SAMPLES)] * 4
            + [weight_spec(U1), weight_spec(V0), feature_spec(2), feature_spec(1), feature_spec(1)],
            out_specs=[
                feature_spec(SAMPLES),
                pl.BlockSpec((TABLES_STEP, BACK_ROWS, EMB), lambda j, at: (j, 0, 0)),
            ],
            scratch_shapes=[pltpu.VMEM((2 * SAMPLES, RANK), BF16)],
        ),
        out_shape=[
            jax.ShapeDtypeStruct((SAMPLES, FEATURES), BF16),
            jax.ShapeDtypeStruct((FIELD_TABLES, BACK_ROWS, EMB), BF16),
        ],
        compiler_params=params(),
        cost_estimate=cost(10**9, 10 * MIB),
    )(at, *quarters, x0, x1, cot, base, weights, weights, bias, sum0, sum1)


def terms_kernel(at, q0, q1, q2, q3, u_side, v_side, own, other, ranks):
    @pl.when(pl.program_id(0) == 0)
    def _():
        read_quarters(at, (q0, q1, q2, q3), ranks)

    is_first = at[AT_CORE] == 0
    for which, side in enumerate((u_side, v_side)):
        rows = ranks[which * SAMPLES : (which + 1) * SAMPLES, :]
        term = dot(rows, side[...], 0, 0).reshape(X_SIZE, Z_SIZE, CORES, SHARE, FEATURE_BLOCK)
        lower, upper = term[:, :, 0], term[:, :, 1]
        own[:, which] = jnp.where(is_first, lower, upper).astype(BF16)
        other[:, which] = jnp.where(is_first, upper, lower).astype(BF16)


GRAD_SHAPE = (X_SIZE, 2, Z_SIZE, SHARE, FEATURES)


def terms(at, quarters, u_side, v_side):
    block = pl.BlockSpec((X_SIZE, 2, Z_SIZE, SHARE, FEATURE_BLOCK), lambda j, at: (0, 0, 0, 0, j))
    return pl.pallas_call(
        terms_kernel,
        grid_spec=pltpu.PrefetchScalarGridSpec(
            num_scalar_prefetch=1,
            grid=(FEATURE_STEPS,),
            in_specs=QUARTER_SPECS + [feature_spec(SAMPLES)] * 2,
            out_specs=[block, block],
            scratch_shapes=[pltpu.VMEM((2 * SAMPLES, RANK), BF16)],
        ),
        out_shape=[jax.ShapeDtypeStruct(GRAD_SHAPE, BF16)] * 2,
        compiler_params=params(),
        cost_estimate=cost(10**9, 6 * MIB),
    )(at, *quarters, u_side, v_side)


def core_sum_kernel(at, *refs):
    for shift in range(X_SIZE):
        mine, theirs, out = refs[shift], refs[X_SIZE + shift], refs[2 * X_SIZE + shift]
        out[...] = (mine[0].astype(F32) + theirs[0].astype(F32)).astype(BF16)


def core_sum(at, own, arrived):
    width = 512

    def spec(shift):
        return pl.BlockSpec(
            (1, 2, Z_SIZE, SHARE, width),
            lambda j, at: (lax.rem(at[AT_X] + shift, X_SIZE), 0, 0, 0, j),
        )

    specs = [spec(shift) for shift in range(X_SIZE)]
    out_spec = pl.BlockSpec((2, Z_SIZE, SHARE, width), lambda j, at: (0, 0, 0, j))
    return pl.pallas_call(
        core_sum_kernel,
        grid_spec=pltpu.PrefetchScalarGridSpec(
            num_scalar_prefetch=1,
            grid=(FEATURES // width,),
            in_specs=specs + specs,
            out_specs=[out_spec] * X_SIZE,
        ),
        out_shape=[jax.ShapeDtypeStruct(GRAD_SHAPE[1:], BF16)] * X_SIZE,
        compiler_params=params(),
        cost_estimate=cost(10**6, 6 * MIB),
    )(at, *([own] * X_SIZE), *([arrived] * X_SIZE))


def x_sum_kernel(at, a, b, c, d, *rest):
    outs, total = rest[:Z_SIZE], rest[Z_SIZE]
    total[...] = (a[...].astype(F32) + b[...].astype(F32)) + (c[...].astype(F32) + d[...].astype(F32))
    for shift, out in enumerate(outs):
        place = lax.rem(at[AT_Z] + shift, Z_SIZE)
        out[...] = total[:, pl.ds(place, 1)].reshape(out.shape).astype(BF16)


def x_sum(at, blocks):
    width = 1024
    in_spec = pl.BlockSpec((2, Z_SIZE, SHARE, width), lambda j, at: (0, 0, 0, j))
    out_spec = pl.BlockSpec((2, SHARE, width), lambda j, at: (0, 0, j))
    return pl.pallas_call(
        x_sum_kernel,
        grid_spec=pltpu.PrefetchScalarGridSpec(
            num_scalar_prefetch=1,
            grid=(FEATURES // width,),
            in_specs=[in_spec] * X_SIZE,
            out_specs=[out_spec] * Z_SIZE,
            scratch_shapes=[pltpu.VMEM((2, Z_SIZE, SHARE, width), F32)],
        ),
        out_shape=[jax.ShapeDtypeStruct((2, SHARE, FEATURES), BF16)] * Z_SIZE,
        compiler_params=params(),
        cost_estimate=cost(10**6, 3 * MIB),
    )(at, *blocks)


def z_sum_kernel(*refs):
    early, late, (grad_u, grad_v) = refs[:Z_SIZE], refs[Z_SIZE : 2 * Z_SIZE], refs[2 * Z_SIZE :]

    def total(blocks, which):
        a, b, c, d = (block[which].astype(F32) for block in blocks)
        return (a + b) + (c + d)

    grad_u[0] = total(early, 0)
    grad_v[1] = total(early, 1)
    grad_u[1] = total(late, 0)
    grad_v[0] = total(late, 1)


def z_sum(early, late):
    return pl.pallas_call(
        z_sum_kernel,
        out_shape=[jax.ShapeDtypeStruct((2, SHARE, FEATURES), F32)] * 2,
        compiler_params=params(),
        cost_estimate=cost(10**6, 2 * MIB),
    )(*early, *late)


def last_kernel(at, back, pooled, proj, grad_pooled, grad_proj, grad_bias):
    step = pl.program_id(0)
    factor = masked_projection(proj, at[AT_WIDTH])
    none = jnp.zeros_like(factor)
    both = jnp.concatenate(
        [jnp.concatenate([factor, none], axis=1), jnp.concatenate([none, factor], axis=1)], axis=0
    )
    total = jnp.zeros((PROJ, EMB), F32)
    bias = jnp.zeros((1, EMB), F32)
    for block in range(back.shape[0]):
        grads = back[block, :HALF, :]
        start = block * SAMPLES
        out = dot(grads, both, 1, 0).astype(BF16)
        grad_pooled[start : start + HALF, :] = out[:, :EMB]
        grad_pooled[start + HALF : start + SAMPLES, :] = out[:, EMB:]
        upper = dot(grads, pooled[start : start + HALF, :], 0, 0)
        lower = dot(grads, pooled[start + HALF : start + SAMPLES, :], 0, 0)
        total += upper[:PROJ] + lower[PROJ:]
        bias += back[block, HALF:, :].astype(F32)[:1]

    @pl.when(step == 0)
    def _():
        grad_proj[...] = total
        grad_bias[...] = bias

    @pl.when(step > 0)
    def _():
        grad_proj[...] += total
        grad_bias[...] += bias


def last(at, back, pooled, proj):
    blocks = 8
    return pl.pallas_call(
        last_kernel,
        grid_spec=pltpu.PrefetchScalarGridSpec(
            num_scalar_prefetch=1,
            grid=(FIELD_TABLES // blocks,),
            in_specs=[
                pl.BlockSpec((blocks, BACK_ROWS, EMB), lambda i, at: (i, 0, 0)),
                pl.BlockSpec((blocks * SAMPLES, EMB), lambda i, at: (i, 0)),
                pl.BlockSpec((1, PROJ, EMB), lambda i, at: (at[AT_BATCH], 0, 0)),
            ],
            out_specs=[
                pl.BlockSpec((blocks * SAMPLES, EMB), lambda i, at: (i, 0)),
                whole_spec(PROJ, EMB),
                whole_spec(1, EMB),
            ],
        ),
        out_shape=[
            jax.ShapeDtypeStruct((TOKENS, EMB), BF16),
            jax.ShapeDtypeStruct((PROJ, EMB), F32),
            jax.ShapeDtypeStruct((1, EMB), F32),
        ],
        compiler_params=params(),
        cost_estimate=cost(10**9, 5 * MIB),
    )(at, back, pooled, proj)


def batch_moves(move):
    pairs = []
    for source in range(X_SIZE * Z_SIZE * CORES):
        x, z, core = source // (Z_SIZE * CORES), source // CORES % Z_SIZE, source % CORES
        x, z, core = move(x, z, core)
        pairs.append((source, (x * Z_SIZE + z) * CORES + core))
    return pairs


def field_moves(move):
    pairs = []
    for source in range(Y_SIZE * HALVES):
        y, half = move(source // HALVES, source % HALVES)
        pairs.append((source, y * HALVES + half))
    return pairs


CORE_SWAP = batch_moves(lambda x, z, core: (x, z, 1 - core))
X_MOVES = [batch_moves(lambda x, z, core, s=s: ((x + s) % X_SIZE, z, core)) for s in range(X_SIZE)]
Z_MOVES = [batch_moves(lambda x, z, core, s=s: (x, (z + s) % Z_SIZE, core)) for s in range(Z_SIZE)]
Y_MOVES = [field_moves(lambda y, half, s=s: ((y + s) % Y_SIZE, half)) for s in range(Y_SIZE)]
HALF_SWAP = field_moves(lambda y, half: (y, 1 - half))


def exchange(parts, axis, moves):
    return [parts[0]] + [lax.ppermute(parts[s], axis, moves[s]) for s in range(1, len(parts))]


def low_sum(parts):
    wide = [part.astype(F32) for part in parts]
    total = wide[0]
    for part in wide[1:]:
        total = total + part
    return total.astype(BF16)


def field_total(parts):
    partial = low_sum(exchange(parts, "field", Y_MOVES))
    whole = low_sum([partial, lax.ppermute(partial, "field", HALF_SWAP)])
    return exchange([whole] * Y_SIZE, "field", Y_MOVES)


def scatter_sum(at, own, other):
    blocks = core_sum(at, own, lax.ppermute(other, "batch", CORE_SWAP))
    blocks = x_sum(at, exchange(blocks, "batch", X_MOVES))
    return exchange(blocks, "batch", Z_MOVES)


def on_device(
    emb_tables, bag_ids, bag_lengths, table_widths, projection, cross_u, cross_v, cross_bias, cotangent
):
    batch = lax.axis_index("batch")
    field = lax.axis_index("field")
    at = jnp.stack(
        [batch, batch // (Z_SIZE * CORES), batch // CORES % Z_SIZE, batch % CORES, field // HALVES, table_widths[0]]
    ).astype(jnp.int32)
    shard = jnp.concatenate([cross_u, cross_v], axis=0)
    weights = lax.all_gather(shard, "batch", axis=0, tiled=True)
    weights = weights.reshape(FIELD_TABLES, 4, SHARE, FEATURES)
    proj = jnp.transpose(projection, (0, 2, 1))

    places = lax.broadcasted_iota(jnp.int32, (BAG, TOKENS), 0)
    ids = jnp.where(places < bag_lengths, bag_ids[0].T, ROWS)
    ids = ids.reshape(BAG, TOKENS // 128, 128).transpose(1, 0, 2).reshape(-1)
    pooled, sent = pool(at, ids, emb_tables[0], proj)
    recv = lax.all_to_all(sent, "batch", split_axis=0, concat_axis=0, tiled=True)

    x0, hg1, sum1, *parts = first(at, recv, cotangent, weights)
    quarters_a = field_total(parts)
    x1, hg0, base, sum0, *parts = second(at, quarters_a, x0, cotangent, weights, cross_bias)
    own_a, other_a = terms(at, quarters_a, hg0, x1)
    quarters_b = field_total(parts)
    early = scatter_sum(at, own_a, other_a)
    crossed, back = third(
        at, quarters_b, x0, x1, cotangent, base, weights, cross_bias, sum0, sum1
    )
    returned = lax.all_to_all(back, "batch", split_axis=0, concat_axis=0, tiled=True)
    own_b, other_b = terms(at, quarters_b, hg1, x0)
    late = scatter_sum(at, own_b, other_b)
    grad_u, grad_v = z_sum(early, late)
    grad_pooled, grad_proj, grad_bias = last(at, returned, pooled, proj)
    return (
        crossed,
        grad_u,
        grad_v,
        grad_bias.reshape(2, PROJ),
        grad_proj.T[None],
        grad_pooled[None],
    )


def solution(mesh):
    return jax.shard_map(
        on_device,
        mesh=mesh,
        in_specs=(
            P(("field", "batch"), None, None),
            P(("field", "batch"), None, None),
            P(("field", "batch"), None),
            P(("field", "batch")),
            P("field", None, None),
            P(None, "batch", "field"),
            P(None, "batch", "field"),
            P(None, "field"),
            P("batch", "field"),
        ),
        out_specs=(
            P("batch", "field"),
            P(None, "batch", "field"),
            P(None, "batch", "field"),
            P(None, ("field", "batch")),
            P(("field", "batch"), None, None),
            P(("field", "batch"), None, None),
        ),
        check_vma=False,
    )
```

```python
import functools

import jax
import jax.numpy as jnp
from jax import lax
from jax.experimental import pallas as pl
from jax.experimental.pallas import tpu as pltpu
from jax.sharding import PartitionSpec as P

BF16 = jnp.bfloat16
F32 = jnp.float32
MIB = 2**20

X_SIZE, Z_SIZE, CORES = 4, 4, 2
Y_SIZE, HALVES = 4, 2

ROWS, EMB, PROJ, BAG = 8192, 128, 64, 8
SAMPLES, FEATURES, RANK = 192, 2048, 512
FIELD_TABLES = 32
HALF = SAMPLES // 2
SHARE = RANK // FIELD_TABLES
TOKENS = SAMPLES * FIELD_TABLES
BACK_ROWS = HALF + 16
FEATURE_BLOCK = 512
POOL_CHUNK = 1536
POOL_UNROLL = 64
QUARTER = 2 * SAMPLES // Y_SIZE

AT_BATCH, AT_X, AT_Z, AT_CORE, AT_Y, AT_WIDTH = range(6)
U0, U1, V0, V1 = range(4)


def params():
    return pltpu.CompilerParams(vmem_limit_bytes=32 * MIB)


def cost(moved):
    return pl.CostEstimate(flops=0, bytes_accessed=moved, transcendentals=0)


def dot(left, right, left_dim, right_dim):
    return lax.dot_general(
        left, right, (((left_dim,), (right_dim,)), ((), ())), preferred_element_type=F32
    )


def masked_projection(proj_ref, width):
    columns = lax.broadcasted_iota(jnp.int32, (PROJ, EMB), 1)
    return jnp.where(columns < width, proj_ref[0].astype(F32), 0.0).astype(BF16)


def pool_kernel(at, ids, table, proj, pooled, sent, wide_table, summed):
    @pl.when(pl.program_id(0) == 0)
    def _():
        within = lax.broadcasted_iota(jnp.int32, (256, EMB), 1) < at[AT_WIDTH]

        @pl.loop(0, ROWS // 256)
        def _(part):
            rows = pl.ds(pl.multiple_of(part * 256, 256), 256)
            wide_table[rows, :] = jnp.where(within, table[rows, :].astype(F32), 0.0)

        wide_table[ROWS : ROWS + 8, :] = jnp.zeros((8, EMB), F32)

    groups = 128 // POOL_UNROLL

    @pl.loop(0, POOL_CHUNK // POOL_UNROLL)
    def _(group):
        first = group * POOL_UNROLL
        base = (group // groups) * (128 * BAG) + (group % groups) * POOL_UNROLL
        for step in range(POOL_UNROLL):
            rows = [wide_table[pl.ds(ids[base + (place * 128 + step)], 1), :] for place in range(BAG)]
            summed[pl.ds(first + step, 1), :] = (
                (rows[0] + rows[1]) + (rows[2] + rows[3])
            ) + ((rows[4] + rows[5]) + (rows[6] + rows[7]))

    low = summed[...].astype(BF16)
    pooled[...] = low
    factor = proj[0]
    none = jnp.zeros_like(factor)
    both = jnp.concatenate(
        [jnp.concatenate([factor, none], axis=1), jnp.concatenate([none, factor], axis=1)], axis=0
    )
    for block in range(POOL_CHUNK // SAMPLES):
        start = block * SAMPLES
        pair = jnp.concatenate(
            [low[start : start + HALF], low[start + HALF : start + SAMPLES]], axis=1
        )
        sent[block] = dot(pair, both, 1, 1).astype(BF16)


def pool(at, ids, table, proj):
    blocks = POOL_CHUNK // SAMPLES
    return pl.pallas_call(
        pool_kernel,
        grid_spec=pltpu.PrefetchScalarGridSpec(
            num_scalar_prefetch=1,
            grid=(TOKENS // POOL_CHUNK,),
            in_specs=[
                pl.BlockSpec((POOL_CHUNK * BAG,), lambda i, at: (i,), memory_space=pltpu.SMEM),
                pl.BlockSpec((ROWS, EMB), lambda i, at: (0, 0)),
                pl.BlockSpec((1, PROJ, EMB), lambda i, at: (at[AT_BATCH], 0, 0)),
            ],
            out_specs=[
                pl.BlockSpec((POOL_CHUNK, EMB), lambda i, at: (i, 0)),
                pl.BlockSpec((blocks, HALF, EMB), lambda i, at: (i, 0, 0)),
            ],
            scratch_shapes=[pltpu.VMEM((ROWS + 8, EMB), F32), pltpu.VMEM((POOL_CHUNK, EMB), F32)],
        ),
        out_shape=[
            jax.ShapeDtypeStruct((TOKENS, EMB), BF16),
            jax.ShapeDtypeStruct((FIELD_TABLES, HALF, EMB), BF16),
        ],
        compiler_params=params(),
        cost_estimate=cost(100 * MIB),
    )(at, ids, table, proj)


def assemble_kernel(at, *refs):
    parts, whole = refs[:-1], refs[-1]
    for shift, part in enumerate(parts):
        place = lax.rem(at[AT_Y] + Y_SIZE - shift, Y_SIZE)
        whole[pl.ds(pl.multiple_of(place * QUARTER, QUARTER), QUARTER), :] = part[...]


def assemble(at, parts):
    return pl.pallas_call(
        assemble_kernel,
        grid_spec=pltpu.PrefetchScalarGridSpec(
            num_scalar_prefetch=1,
            grid=(1,),
            in_specs=[whole_spec(QUARTER, RANK)] * Y_SIZE,
            out_specs=whole_spec(2 * SAMPLES, RANK),
        ),
        out_shape=jax.ShapeDtypeStruct((2 * SAMPLES, RANK), BF16),
        compiler_params=params(),
        cost_estimate=cost(MIB),
    )(at, *parts)


def write_quarters(at, total, parts):
    for shift, part in enumerate(parts):
        place = lax.rem(at[AT_Y] + shift, Y_SIZE)
        part[...] = total[pl.ds(pl.multiple_of(place * QUARTER, QUARTER), QUARTER), :].astype(BF16)


def weight(ref):
    return ref[...].reshape(RANK, FEATURE_BLOCK)


def first_kernel(at, recv, cot, v0, u1, pair, bias_out, q0, q1, q2, q3, total):
    step = pl.program_id(0)
    columns = []
    for place in range(FEATURE_BLOCK // EMB):
        left, right = recv[2 * place], recv[2 * place + 1]
        top = jnp.concatenate([left[:, :PROJ], right[:, :PROJ]], axis=1)
        bottom = jnp.concatenate([left[:, PROJ:], right[:, PROJ:]], axis=1)
        columns.append(jnp.concatenate([top, bottom], axis=0))
    x0 = jnp.concatenate(columns, axis=1)
    hg = (cot[...].astype(F32) * x0.astype(F32)).astype(BF16)
    pair[0] = hg
    pair[1] = x0
    bias_out[...] = jnp.sum(hg.astype(F32), axis=0, keepdims=True)
    rank = dot(x0, weight(v0), 1, 1)
    rank_grad = dot(hg, weight(u1), 1, 1)

    @pl.when(step == 0)
    def _():
        total[:SAMPLES, :] = rank
        total[SAMPLES:, :] = rank_grad

    @pl.when(step > 0)
    def _():
        total[:SAMPLES, :] += rank
        total[SAMPLES:, :] += rank_grad

    @pl.when(step == pl.num_programs(0) - 1)
    def _():
        write_quarters(at, total, (q0, q1, q2, q3))


def feature_spec(rows):
    return pl.BlockSpec((rows, FEATURE_BLOCK), lambda j, at: (0, j))


def weight_spec(which):
    return pl.BlockSpec(
        (FIELD_TABLES, 1, SHARE, FEATURE_BLOCK), lambda j, at: (0, which, 0, j)
    )


def whole_spec(*shape):
    return pl.BlockSpec(shape, lambda j, at: (0,) * len(shape))


def pair_spec(which=None):
    if which is None:
        return pl.BlockSpec((2, SAMPLES, FEATURE_BLOCK), lambda j, at: (0, 0, j))
    return pl.BlockSpec((None, SAMPLES, FEATURE_BLOCK), lambda j, at: (which, 0, j))


QUARTER_SPECS = [whole_spec(QUARTER, RANK)] * Y_SIZE
QUARTER_SHAPES = [jax.ShapeDtypeStruct((QUARTER, RANK), BF16)] * Y_SIZE
FEATURE_STEPS = FEATURES // FEATURE_BLOCK
TABLES_STEP = FEATURE_BLOCK // PROJ


def first(at, recv, cot, weights):
    return pl.pallas_call(
        first_kernel,
        grid_spec=pltpu.PrefetchScalarGridSpec(
            num_scalar_prefetch=1,
            grid=(FEATURE_STEPS,),
            in_specs=[
                pl.BlockSpec((TABLES_STEP, HALF, EMB), lambda j, at: (j, 0, 0)),
                feature_spec(SAMPLES),
                weight_spec(V0),
                weight_spec(U1),
            ],
            out_specs=[pair_spec(), feature_spec(1)] + QUARTER_SPECS,
            scratch_shapes=[pltpu.VMEM((2 * SAMPLES, RANK), F32)],
        ),
        out_shape=[
            jax.ShapeDtypeStruct((2, SAMPLES, FEATURES), BF16),
            jax.ShapeDtypeStruct((1, FEATURES), F32),
        ]
        + QUARTER_SHAPES,
        compiler_params=params(),
        cost_estimate=cost(8 * MIB),
    )(at, recv, cot, weights, weights)


def second_kernel(at, ranks, x0_ref, cot, u0_ref, v1_ref, bias, pair, base_out, bias_out, q0, q1, q2, q3, total):
    step = pl.program_id(0)
    u0, v1 = weight(u0_ref), weight(v1_ref)
    x0 = x0_ref[...].astype(F32)
    hidden = dot(ranks[:SAMPLES, :], u0, 1, 0) + bias[0:1, :]
    upstream = cot[...].astype(F32) + dot(ranks[SAMPLES:, :], v1, 1, 0)
    x1 = (x0 * hidden + x0).astype(BF16)
    hg = (upstream * x0).astype(BF16)
    pair[0] = hg
    pair[1] = x1
    base_out[...] = upstream + upstream * hidden
    bias_out[...] = jnp.sum(hg.astype(F32), axis=0, keepdims=True)
    rank = dot(x1, v1, 1, 1)
    rank_grad = dot(hg, u0, 1, 1)

    @pl.when(step == 0)
    def _():
        total[:SAMPLES, :] = rank
        total[SAMPLES:, :] = rank_grad

    @pl.when(step > 0)
    def _():
        total[:SAMPLES, :] += rank
        total[SAMPLES:, :] += rank_grad

    @pl.when(step == pl.num_programs(0) - 1)
    def _():
        write_quarters(at, total, (q0, q1, q2, q3))


def second(at, ranks, pair, cot, weights, bias):
    return pl.pallas_call(
        second_kernel,
        grid_spec=pltpu.PrefetchScalarGridSpec(
            num_scalar_prefetch=1,
            grid=(FEATURE_STEPS,),
            in_specs=[
                whole_spec(2 * SAMPLES, RANK),
                pair_spec(1),
                feature_spec(SAMPLES),
                weight_spec(U0),
                weight_spec(V1),
                feature_spec(2),
            ],
            out_specs=[
                pair_spec(),
                feature_spec(SAMPLES),
                feature_spec(1),
            ]
            + QUARTER_SPECS,
            scratch_shapes=[pltpu.VMEM((2 * SAMPLES, RANK), F32)],
        ),
        out_shape=[
            jax.ShapeDtypeStruct((2, SAMPLES, FEATURES), BF16),
            jax.ShapeDtypeStruct((SAMPLES, FEATURES), F32),
            jax.ShapeDtypeStruct((1, FEATURES), F32),
        ]
        + QUARTER_SHAPES,
        compiler_params=params(),
        cost_estimate=cost(10 * MIB),
    )(at, ranks, pair, cot, weights, weights, bias)


def third_kernel(at, ranks, x0_ref, x1_ref, cot, base, u1_ref, v0_ref, bias, sum0, sum1, crossed, back):
    hidden = dot(ranks[:SAMPLES, :], weight(u1_ref), 1, 0) + bias[1:2, :]
    crossed[...] = (x0_ref[...].astype(F32) * hidden + x1_ref[...].astype(F32)).astype(BF16)
    grad = base[...] + dot(ranks[SAMPLES:, :], weight(v0_ref), 1, 0) + cot[...].astype(F32) * hidden
    grad = grad.astype(BF16)
    for table in range(TABLES_STEP):
        columns = slice(table * PROJ, (table + 1) * PROJ)
        back[table, :HALF, :] = jnp.concatenate([grad[:HALF, columns], grad[HALF:, columns]], axis=1)
        row = jnp.concatenate([sum0[:, columns], sum1[:, columns]], axis=1)
        first_row = lax.broadcasted_iota(jnp.int32, (16, EMB), 0) == 0
        back[table, HALF:, :] = jnp.where(first_row, row, 0.0).astype(BF16)


def third(at, ranks, pair_0, pair_1, cot, base, weights, bias, sum0, sum1):
    return pl.pallas_call(
        third_kernel,
        grid_spec=pltpu.PrefetchScalarGridSpec(
            num_scalar_prefetch=1,
            grid=(FEATURE_STEPS,),
            in_specs=[whole_spec(2 * SAMPLES, RANK), pair_spec(1), pair_spec(1)]
            + [feature_spec(SAMPLES)] * 2
            + [weight_spec(U1), weight_spec(V0), feature_spec(2), feature_spec(1), feature_spec(1)],
            out_specs=[
                feature_spec(SAMPLES),
                pl.BlockSpec((TABLES_STEP, BACK_ROWS, EMB), lambda j, at: (j, 0, 0)),
            ],
        ),
        out_shape=[
            jax.ShapeDtypeStruct((SAMPLES, FEATURES), BF16),
            jax.ShapeDtypeStruct((FIELD_TABLES, BACK_ROWS, EMB), BF16),
        ],
        compiler_params=params(),
        cost_estimate=cost(MIB),
    )(at, ranks, pair_0, pair_1, cot, base, weights, weights, bias, sum0, sum1)


def terms_kernel(at, ranks, other_ranks, pair, other_pair, out, sides):
    @pl.when(pl.program_id(0) == 0)
    def _():
        is_first = at[AT_CORE] == 0
        for which in range(2):
            part = slice(which * SAMPLES, (which + 1) * SAMPLES)
            rows = jnp.concatenate([ranks[part, :], other_ranks[part, :]], axis=0).astype(F32)
            turned = rows.T.reshape(RANK // (CORES * SHARE), CORES, SHARE, 2 * SAMPLES)
            mine = jnp.where(is_first, turned[:, 0], turned[:, 1])
            sides[which] = mine.reshape(RANK // CORES, 2 * SAMPLES).astype(BF16)

    for which in range(2):
        side = jnp.concatenate([pair[which], other_pair[which]], axis=0)
        term = dot(sides[which], side, 1, 0).astype(BF16)
        out[:, :, which] = term.reshape(X_SIZE, Z_SIZE, SHARE, FEATURE_BLOCK)


GRAD_SHAPE = (X_SIZE, Z_SIZE, 2, SHARE, FEATURES)


def terms(at, ranks, other_ranks, pair, other_pair):
    return pl.pallas_call(
        terms_kernel,
        grid_spec=pltpu.PrefetchScalarGridSpec(
            num_scalar_prefetch=1,
            grid=(FEATURE_STEPS,),
            in_specs=[whole_spec(2 * SAMPLES, RANK)] * 2 + [pair_spec()] * 2,
            out_specs=pl.BlockSpec(GRAD_SHAPE[:-1] + (FEATURE_BLOCK,), lambda j, at: (0, 0, 0, 0, j)),
            scratch_shapes=[pltpu.VMEM((2, RANK // CORES, 2 * SAMPLES), BF16)],
        ),
        out_shape=jax.ShapeDtypeStruct(GRAD_SHAPE, BF16),
        compiler_params=params(),
        cost_estimate=cost(6 * MIB),
    )(at, ranks, other_ranks, pair, other_pair)


def z_sum_kernel(early, late, grad_u, grad_v):
    def total(blocks, which):
        a, b, c, d = (blocks[place, which].astype(F32) for place in range(Z_SIZE))
        return (a + b) + (c + d)

    grad_u[0] = total(early, 0)
    grad_v[1] = total(early, 1)
    grad_u[1] = total(late, 0)
    grad_v[0] = total(late, 1)


def z_sum(early, late):
    return pl.pallas_call(
        z_sum_kernel,
        out_shape=[jax.ShapeDtypeStruct((2, SHARE, FEATURES), F32)] * 2,
        compiler_params=params(),
        cost_estimate=cost(2 * MIB),
    )(early, late)


def last_kernel(at, back, pooled, proj, grad_pooled, grad_proj, grad_bias):
    step = pl.program_id(0)
    factor = masked_projection(proj, at[AT_WIDTH])
    none = jnp.zeros_like(factor)
    both = jnp.concatenate(
        [jnp.concatenate([factor, none], axis=1), jnp.concatenate([none, factor], axis=1)], axis=0
    )
    total = jnp.zeros((PROJ, EMB), F32)
    bias = jnp.zeros((1, EMB), F32)
    for block in range(back.shape[0]):
        grads = back[block, :HALF, :]
        start = block * SAMPLES
        out = dot(grads, both, 1, 0).astype(BF16)
        grad_pooled[start : start + HALF, :] = out[:, :EMB]
        grad_pooled[start + HALF : start + SAMPLES, :] = out[:, EMB:]
        upper = dot(grads, pooled[start : start + HALF, :], 0, 0)
        lower = dot(grads, pooled[start + HALF : start + SAMPLES, :], 0, 0)
        total += upper[:PROJ] + lower[PROJ:]
        bias += back[block, HALF:, :].astype(F32)[:1]

    @pl.when(step == 0)
    def _():
        grad_proj[...] = total
        grad_bias[...] = bias

    @pl.when(step > 0)
    def _():
        grad_proj[...] += total
        grad_bias[...] += bias


def last(at, back, pooled, proj):
    blocks = 8
    return pl.pallas_call(
        last_kernel,
        grid_spec=pltpu.PrefetchScalarGridSpec(
            num_scalar_prefetch=1,
            grid=(FIELD_TABLES // blocks,),
            in_specs=[
                pl.BlockSpec((blocks, BACK_ROWS, EMB), lambda i, at: (i, 0, 0)),
                pl.BlockSpec((blocks * SAMPLES, EMB), lambda i, at: (i, 0)),
                pl.BlockSpec((1, PROJ, EMB), lambda i, at: (at[AT_BATCH], 0, 0)),
            ],
            out_specs=[
                pl.BlockSpec((blocks * SAMPLES, EMB), lambda i, at: (i, 0)),
                whole_spec(PROJ, EMB),
                whole_spec(1, EMB),
            ],
        ),
        out_shape=[
            jax.ShapeDtypeStruct((TOKENS, EMB), BF16),
            jax.ShapeDtypeStruct((PROJ, EMB), F32),
            jax.ShapeDtypeStruct((1, EMB), F32),
        ],
        compiler_params=params(),
        cost_estimate=cost(5 * MIB),
    )(at, back, pooled, proj)


def batch_moves(move):
    pairs = []
    for source in range(X_SIZE * Z_SIZE * CORES):
        x, z, core = source // (Z_SIZE * CORES), source // CORES % Z_SIZE, source % CORES
        x, z, core = move(x, z, core)
        pairs.append((source, (x * Z_SIZE + z) * CORES + core))
    return pairs


def field_moves(move):
    pairs = []
    for source in range(Y_SIZE * HALVES):
        y, half = move(source // HALVES, source % HALVES)
        pairs.append((source, y * HALVES + half))
    return pairs


CORE_SWAP = batch_moves(lambda x, z, core: (x, z, 1 - core))
X_GROUPS = [
    [(x * Z_SIZE + z) * CORES + core for x in range(X_SIZE)] for z in range(Z_SIZE) for core in range(CORES)
]
Z_GROUPS = [
    [(x * Z_SIZE + z) * CORES + core for z in range(Z_SIZE)] for x in range(X_SIZE) for core in range(CORES)
]
Y_MOVES = [field_moves(lambda y, half, s=s: ((y + s) % Y_SIZE, half)) for s in range(Y_SIZE)]
HALF_SWAP = field_moves(lambda y, half: (y, 1 - half))


def exchange(parts, axis, moves):
    return [parts[0]] + [lax.ppermute(parts[s], axis, moves[s]) for s in range(1, len(parts))]


def scatter_sum(blocks, groups):
    return lax.psum_scatter(
        blocks, "batch", scatter_dimension=0, tiled=True, axis_index_groups=groups
    )


def low_sum(parts):
    wide = [part.astype(F32) for part in parts]
    total = wide[0]
    for part in wide[1:]:
        total = total + part
    return total.astype(BF16)


def to_all(blocks, axis, groups=None):
    return lax.all_to_all(
        blocks, axis, split_axis=0, concat_axis=0, tiled=True, axis_index_groups=groups
    )


def in_hbm(value):
    return pltpu.with_memory_space_constraint(value, pltpu.HBM)


def after(value, earlier):
    return lax.optimization_barrier((value, earlier))[0]


def core_swap(value):
    return lax.ppermute(value, "batch", CORE_SWAP)


def both_halves(partial):
    return low_sum([partial, lax.ppermute(partial, "field", HALF_SWAP)])


def on_device(
    emb_tables, bag_ids, bag_lengths, table_widths, projection, cross_u, cross_v, cross_bias, cotangent
):
    batch = lax.axis_index("batch")
    field = lax.axis_index("field")
    at = jnp.stack(
        [batch, batch // (Z_SIZE * CORES), batch // CORES % Z_SIZE, batch % CORES, field // HALVES, table_widths[0]]
    ).astype(jnp.int32)
    shard = jnp.concatenate([cross_u, cross_v], axis=0)
    weights = lax.all_gather(shard, "batch", axis=0, tiled=True)
    weights = in_hbm(weights.reshape(FIELD_TABLES, 4, SHARE, FEATURES))
    proj = jnp.transpose(projection, (0, 2, 1))

    places = lax.broadcasted_iota(jnp.int32, (BAG, TOKENS), 0)
    ids = jnp.where(places < bag_lengths, bag_ids[0].T, ROWS)
    ids = ids.reshape(BAG, TOKENS // 128, 128).transpose(1, 0, 2).reshape(-1)
    pooled, sent = pool(at, ids, in_hbm(emb_tables[0]), proj)
    recv = to_all(sent, "batch")

    pair_0, sum1, *parts = first(at, recv, cotangent, weights)
    other_0 = core_swap(pair_0)
    parts = exchange(parts, "field", Y_MOVES)
    partial = low_sum([after(parts[0], other_0)] + parts[1:])
    ranks = assemble(at, exchange([both_halves(partial)] * Y_SIZE, "field", Y_MOVES))
    other_ranks = core_swap(ranks)

    pair_1, base, sum0, *parts = second(at, ranks, pair_0, cotangent, weights, cross_bias)
    blocks = terms(at, ranks, other_ranks, pair_1, core_swap(pair_1))
    early = scatter_sum(blocks, X_GROUPS)[0]
    parts = exchange(parts, "field", Y_MOVES)
    partial = low_sum([after(parts[0], blocks)] + parts[1:])
    ranks = assemble(at, exchange([both_halves(partial)] * Y_SIZE, "field", Y_MOVES))

    blocks = terms(at, ranks, core_swap(ranks), pair_0, other_0)
    crossed, back = third(
        at, after(ranks, blocks), pair_0, pair_1, cotangent, base, weights, cross_bias, sum0, sum1
    )
    early = to_all(early, "batch", Z_GROUPS)
    returned = to_all(after(back, early), "batch")
    late = scatter_sum(blocks, X_GROUPS)[0]
    late = to_all(after(late, returned), "batch", Z_GROUPS)
    grad_u, grad_v = z_sum(early, late)
    grad_pooled, grad_proj, grad_bias = last(at, returned, pooled, proj)
    return (
        crossed,
        grad_u,
        grad_v,
        grad_bias.reshape(2, PROJ),
        grad_proj.T[None],
        grad_pooled[None],
    )


def solution(mesh):
    return jax.shard_map(
        on_device,
        mesh=mesh,
        in_specs=(
            P(("field", "batch"), None, None),
            P(("field", "batch"), None, None),
            P(("field", "batch"), None),
            P(("field", "batch")),
            P("field", None, None),
            P(None, "batch", "field"),
            P(None, "batch", "field"),
            P(None, "field"),
            P("batch", "field"),
        ),
        out_specs=(
            P("batch", "field"),
            P(None, "batch", "field"),
            P(None, "batch", "field"),
            P(None, ("field", "batch")),
            P(("field", "batch"), None, None),
            P(("field", "batch"), None, None),
        ),
        check_vma=False,
    )
```

```python
import functools

import jax
import jax.numpy as jnp
from jax import lax
from jax.experimental import pallas as pl
from jax.experimental.pallas import tpu as pltpu
from jax.sharding import PartitionSpec as P

BF16 = jnp.bfloat16
F32 = jnp.float32
MIB = 2**20

X_SIZE, Z_SIZE, CORES = 4, 4, 2
Y_SIZE, HALVES = 4, 2

ROWS, EMB, PROJ, BAG = 8192, 128, 64, 8
SAMPLES, FEATURES, RANK = 192, 2048, 512
FIELD_TABLES = 32
HALF = SAMPLES // 2
SHARE = RANK // FIELD_TABLES
TOKENS = SAMPLES * FIELD_TABLES
BACK_ROWS = HALF + 16
FEATURE_BLOCK = 512
POOL_CHUNK = 1536
POOL_UNROLL = 64
QUARTER = 2 * SAMPLES // Y_SIZE

AT_BATCH, AT_X, AT_Z, AT_CORE, AT_Y, AT_WIDTH = range(6)
U0, U1, V0, V1 = range(4)


def params():
    return pltpu.CompilerParams(vmem_limit_bytes=32 * MIB)


def cost(moved):
    return pl.CostEstimate(flops=0, bytes_accessed=moved, transcendentals=0)


def dot(left, right, left_dim, right_dim):
    return lax.dot_general(
        left, right, (((left_dim,), (right_dim,)), ((), ())), preferred_element_type=F32
    )


def masked_projection(proj_ref, width):
    columns = lax.broadcasted_iota(jnp.int32, (PROJ, EMB), 1)
    return jnp.where(columns < width, proj_ref[0].astype(F32), 0.0).astype(BF16)


def pool_kernel(at, ids, table, proj, pooled, sent, wide_table, summed):
    @pl.when(pl.program_id(0) == 0)
    def _():
        within = lax.broadcasted_iota(jnp.int32, (256, EMB), 1) < at[AT_WIDTH]

        @pl.loop(0, ROWS // 256)
        def _(part):
            rows = pl.ds(pl.multiple_of(part * 256, 256), 256)
            wide_table[rows, :] = jnp.where(within, table[rows, :].astype(F32), 0.0)

        wide_table[ROWS : ROWS + 8, :] = jnp.zeros((8, EMB), F32)

    groups = 128 // POOL_UNROLL

    @pl.loop(0, POOL_CHUNK // POOL_UNROLL)
    def _(group):
        first = group * POOL_UNROLL
        base = (group // groups) * (128 * BAG) + (group % groups) * POOL_UNROLL
        for step in range(POOL_UNROLL):
            rows = [wide_table[pl.ds(ids[base + (place * 128 + step)], 1), :] for place in range(BAG)]
            summed[pl.ds(first + step, 1), :] = (
                (rows[0] + rows[1]) + (rows[2] + rows[3])
            ) + ((rows[4] + rows[5]) + (rows[6] + rows[7]))

    low = summed[...].astype(BF16)
    pooled[...] = low
    factor = proj[0]
    none = jnp.zeros_like(factor)
    both = jnp.concatenate(
        [jnp.concatenate([factor, none], axis=1), jnp.concatenate([none, factor], axis=1)], axis=0
    )
    for block in range(POOL_CHUNK // SAMPLES):
        start = block * SAMPLES
        pair = jnp.concatenate(
            [low[start : start + HALF], low[start + HALF : start + SAMPLES]], axis=1
        )
        sent[block] = dot(pair, both, 1, 1).astype(BF16)


def pool(at, ids, table, proj):
    blocks = POOL_CHUNK // SAMPLES
    return pl.pallas_call(
        pool_kernel,
        grid_spec=pltpu.PrefetchScalarGridSpec(
            num_scalar_prefetch=1,
            grid=(TOKENS // POOL_CHUNK,),
            in_specs=[
                pl.BlockSpec((POOL_CHUNK * BAG,), lambda i, at: (i,), memory_space=pltpu.SMEM),
                pl.BlockSpec((ROWS, EMB), lambda i, at: (0, 0)),
                pl.BlockSpec((1, PROJ, EMB), lambda i, at: (at[AT_BATCH], 0, 0)),
            ],
            out_specs=[
                pl.BlockSpec((POOL_CHUNK, EMB), lambda i, at: (i, 0)),
                pl.BlockSpec((blocks, HALF, EMB), lambda i, at: (i, 0, 0)),
            ],
            scratch_shapes=[pltpu.VMEM((ROWS + 8, EMB), F32), pltpu.VMEM((POOL_CHUNK, EMB), F32)],
        ),
        out_shape=[
            jax.ShapeDtypeStruct((TOKENS, EMB), BF16),
            jax.ShapeDtypeStruct((FIELD_TABLES, HALF, EMB), BF16),
        ],
        compiler_params=params(),
        cost_estimate=cost(100 * MIB),
    )(at, ids, table, proj)


def assemble_kernel(at, *refs):
    parts, whole = refs[:-1], refs[-1]
    for shift, part in enumerate(parts):
        place = lax.rem(at[AT_Y] + Y_SIZE - shift, Y_SIZE)
        whole[pl.ds(pl.multiple_of(place * QUARTER, QUARTER), QUARTER), :] = part[...]


def assemble(at, parts):
    return pl.pallas_call(
        assemble_kernel,
        grid_spec=pltpu.PrefetchScalarGridSpec(
            num_scalar_prefetch=1,
            grid=(1,),
            in_specs=[whole_spec(QUARTER, RANK)] * Y_SIZE,
            out_specs=whole_spec(2 * SAMPLES, RANK),
        ),
        out_shape=jax.ShapeDtypeStruct((2 * SAMPLES, RANK), BF16),
        compiler_params=params(),
        cost_estimate=cost(MIB),
    )(at, *parts)


def write_quarters(at, total, parts):
    for shift, part in enumerate(parts):
        place = lax.rem(at[AT_Y] + shift, Y_SIZE)
        part[...] = total[pl.ds(pl.multiple_of(place * QUARTER, QUARTER), QUARTER), :].astype(BF16)


def weight(ref):
    return ref[...].reshape(RANK, FEATURE_BLOCK)


def unpack_kernel(recv, cot, pair, bias_out):
    columns = []
    for place in range(FEATURE_BLOCK // EMB):
        left, right = recv[2 * place], recv[2 * place + 1]
        top = jnp.concatenate([left[:, :PROJ], right[:, :PROJ]], axis=1)
        bottom = jnp.concatenate([left[:, PROJ:], right[:, PROJ:]], axis=1)
        columns.append(jnp.concatenate([top, bottom], axis=0))
    x0 = jnp.concatenate(columns, axis=1)
    hg = (cot[...].astype(F32) * x0.astype(F32)).astype(BF16)
    pair[0] = hg
    pair[1] = x0
    bias_out[...] = jnp.sum(hg.astype(F32), axis=0, keepdims=True)


def unpack(recv, cot):
    return pl.pallas_call(
        unpack_kernel,
        grid=(FEATURE_STEPS,),
        in_specs=[
            pl.BlockSpec((TABLES_STEP, HALF, EMB), lambda j: (j, 0, 0)),
            pl.BlockSpec((SAMPLES, FEATURE_BLOCK), lambda j: (0, j)),
        ],
        out_specs=[
            pl.BlockSpec((2, SAMPLES, FEATURE_BLOCK), lambda j: (0, 0, j)),
            pl.BlockSpec((1, FEATURE_BLOCK), lambda j: (0, j)),
        ],
        out_shape=[
            jax.ShapeDtypeStruct((2, SAMPLES, FEATURES), BF16),
            jax.ShapeDtypeStruct((1, FEATURES), F32),
        ],
        compiler_params=params(),
        cost_estimate=cost(4 * MIB),
    )(recv, cot)


def first_kernel(at, pair, v0, u1, q0, q1, q2, q3, total):
    step = pl.program_id(0)
    rank = dot(pair[1], weight(v0), 1, 1)
    rank_grad = dot(pair[0], weight(u1), 1, 1)

    @pl.when(step == 0)
    def _():
        total[:SAMPLES, :] = rank
        total[SAMPLES:, :] = rank_grad

    @pl.when(step > 0)
    def _():
        total[:SAMPLES, :] += rank
        total[SAMPLES:, :] += rank_grad

    @pl.when(step == pl.num_programs(0) - 1)
    def _():
        write_quarters(at, total, (q0, q1, q2, q3))


def feature_spec(rows):
    return pl.BlockSpec((rows, FEATURE_BLOCK), lambda j, at: (0, j))


def weight_spec(which):
    return pl.BlockSpec(
        (FIELD_TABLES, 1, SHARE, FEATURE_BLOCK), lambda j, at: (0, which, 0, j)
    )


def whole_spec(*shape):
    return pl.BlockSpec(shape, lambda j, at: (0,) * len(shape))


def pair_spec(which=None):
    if which is None:
        return pl.BlockSpec((2, SAMPLES, FEATURE_BLOCK), lambda j, at: (0, 0, j))
    return pl.BlockSpec((None, SAMPLES, FEATURE_BLOCK), lambda j, at: (which, 0, j))


QUARTER_SPECS = [whole_spec(QUARTER, RANK)] * Y_SIZE
QUARTER_SHAPES = [jax.ShapeDtypeStruct((QUARTER, RANK), BF16)] * Y_SIZE
FEATURE_STEPS = FEATURES // FEATURE_BLOCK
TABLES_STEP = FEATURE_BLOCK // PROJ


def first(at, pair, weights):
    return pl.pallas_call(
        first_kernel,
        grid_spec=pltpu.PrefetchScalarGridSpec(
            num_scalar_prefetch=1,
            grid=(FEATURE_STEPS,),
            in_specs=[pair_spec(), weight_spec(V0), weight_spec(U1)],
            out_specs=QUARTER_SPECS,
            scratch_shapes=[pltpu.VMEM((2 * SAMPLES, RANK), F32)],
        ),
        out_shape=QUARTER_SHAPES,
        compiler_params=params(),
        cost_estimate=cost(8 * MIB),
    )(at, pair, weights, weights)


def second_kernel(at, ranks, x0_ref, cot, u0_ref, v1_ref, bias, pair, base_out, bias_out, q0, q1, q2, q3, total):
    step = pl.program_id(0)
    u0, v1 = weight(u0_ref), weight(v1_ref)
    x0 = x0_ref[...].astype(F32)
    hidden = dot(ranks[:SAMPLES, :], u0, 1, 0) + bias[0:1, :]
    upstream = cot[...].astype(F32) + dot(ranks[SAMPLES:, :], v1, 1, 0)
    x1 = (x0 * hidden + x0).astype(BF16)
    hg = (upstream * x0).astype(BF16)
    pair[0] = hg
    pair[1] = x1
    base_out[...] = upstream + upstream * hidden
    bias_out[...] = jnp.sum(hg.astype(F32), axis=0, keepdims=True)
    rank = dot(x1, v1, 1, 1)
    rank_grad = dot(hg, u0, 1, 1)

    @pl.when(step == 0)
    def _():
        total[:SAMPLES, :] = rank
        total[SAMPLES:, :] = rank_grad

    @pl.when(step > 0)
    def _():
        total[:SAMPLES, :] += rank
        total[SAMPLES:, :] += rank_grad

    @pl.when(step == pl.num_programs(0) - 1)
    def _():
        write_quarters(at, total, (q0, q1, q2, q3))


def second(at, ranks, pair, cot, weights, bias):
    return pl.pallas_call(
        second_kernel,
        grid_spec=pltpu.PrefetchScalarGridSpec(
            num_scalar_prefetch=1,
            grid=(FEATURE_STEPS,),
            in_specs=[
                whole_spec(2 * SAMPLES, RANK),
                pair_spec(1),
                feature_spec(SAMPLES),
                weight_spec(U0),
                weight_spec(V1),
                feature_spec(2),
            ],
            out_specs=[
                pair_spec(),
                feature_spec(SAMPLES),
                feature_spec(1),
            ]
            + QUARTER_SPECS,
            scratch_shapes=[pltpu.VMEM((2 * SAMPLES, RANK), F32)],
        ),
        out_shape=[
            jax.ShapeDtypeStruct((2, SAMPLES, FEATURES), BF16),
            jax.ShapeDtypeStruct((SAMPLES, FEATURES), F32),
            jax.ShapeDtypeStruct((1, FEATURES), F32),
        ]
        + QUARTER_SHAPES,
        compiler_params=params(),
        cost_estimate=cost(10 * MIB),
    )(at, ranks, pair, cot, weights, weights, bias)


def third_kernel(at, ranks, x0_ref, x1_ref, cot, base, u1_ref, v0_ref, bias, sum0, sum1, crossed, back):
    hidden = dot(ranks[:SAMPLES, :], weight(u1_ref), 1, 0) + bias[1:2, :]
    crossed[...] = (x0_ref[...].astype(F32) * hidden + x1_ref[...].astype(F32)).astype(BF16)
    grad = base[...] + dot(ranks[SAMPLES:, :], weight(v0_ref), 1, 0) + cot[...].astype(F32) * hidden
    grad = grad.astype(BF16)
    for table in range(TABLES_STEP):
        columns = slice(table * PROJ, (table + 1) * PROJ)
        back[table, :HALF, :] = jnp.concatenate([grad[:HALF, columns], grad[HALF:, columns]], axis=1)
        row = jnp.concatenate([sum0[:, columns], sum1[:, columns]], axis=1)
        first_row = lax.broadcasted_iota(jnp.int32, (16, EMB), 0) == 0
        back[table, HALF:, :] = jnp.where(first_row, row, 0.0).astype(BF16)


def third(at, ranks, pair_0, pair_1, cot, base, weights, bias, sum0, sum1):
    return pl.pallas_call(
        third_kernel,
        grid_spec=pltpu.PrefetchScalarGridSpec(
            num_scalar_prefetch=1,
            grid=(FEATURE_STEPS,),
            in_specs=[whole_spec(2 * SAMPLES, RANK), pair_spec(1), pair_spec(1)]
            + [feature_spec(SAMPLES)] * 2
            + [weight_spec(U1), weight_spec(V0), feature_spec(2), feature_spec(1), feature_spec(1)],
            out_specs=[
                feature_spec(SAMPLES),
                pl.BlockSpec((TABLES_STEP, BACK_ROWS, EMB), lambda j, at: (j, 0, 0)),
            ],
        ),
        out_shape=[
            jax.ShapeDtypeStruct((SAMPLES, FEATURES), BF16),
            jax.ShapeDtypeStruct((FIELD_TABLES, BACK_ROWS, EMB), BF16),
        ],
        compiler_params=params(),
        cost_estimate=cost(MIB),
    )(at, ranks, pair_0, pair_1, cot, base, weights, weights, bias, sum0, sum1)


def terms_kernel(at, ranks, other_ranks, pair, other_pair, out, sides):
    @pl.when(pl.program_id(0) == 0)
    def _():
        is_first = at[AT_CORE] == 0
        for which in range(2):
            part = slice(which * SAMPLES, (which + 1) * SAMPLES)
            rows = jnp.concatenate([ranks[part, :], other_ranks[part, :]], axis=0).astype(F32)
            turned = rows.T.reshape(RANK // (CORES * SHARE), CORES, SHARE, 2 * SAMPLES)
            mine = jnp.where(is_first, turned[:, 0], turned[:, 1])
            sides[which] = mine.reshape(RANK // CORES, 2 * SAMPLES).astype(BF16)

    for which in range(2):
        side = jnp.concatenate([pair[which], other_pair[which]], axis=0)
        term = dot(sides[which], side, 1, 0).astype(BF16)
        out[:, :, which] = term.reshape(X_SIZE, Z_SIZE, SHARE, FEATURE_BLOCK)


GRAD_SHAPE = (X_SIZE, Z_SIZE, 2, SHARE, FEATURES)


def terms(at, ranks, other_ranks, pair, other_pair):
    return pl.pallas_call(
        terms_kernel,
        grid_spec=pltpu.PrefetchScalarGridSpec(
            num_scalar_prefetch=1,
            grid=(FEATURE_STEPS,),
            in_specs=[whole_spec(2 * SAMPLES, RANK)] * 2 + [pair_spec()] * 2,
            out_specs=pl.BlockSpec(GRAD_SHAPE[:-1] + (FEATURE_BLOCK,), lambda j, at: (0, 0, 0, 0, j)),
            scratch_shapes=[pltpu.VMEM((2, RANK // CORES, 2 * SAMPLES), BF16)],
        ),
        out_shape=jax.ShapeDtypeStruct(GRAD_SHAPE, BF16),
        compiler_params=params(),
        cost_estimate=cost(6 * MIB),
    )(at, ranks, other_ranks, pair, other_pair)


def z_split_kernel(at, blocks, *outs):
    for shift, out in enumerate(outs):
        out[...] = blocks[lax.rem(at[AT_Z] + shift, Z_SIZE)]


def z_split(at, blocks):
    return pl.pallas_call(
        z_split_kernel,
        grid_spec=pltpu.PrefetchScalarGridSpec(
            num_scalar_prefetch=1,
            grid=(1,),
            in_specs=[whole_spec(*GRAD_SHAPE[1:])],
            out_specs=[whole_spec(2, SHARE, FEATURES)] * Z_SIZE,
        ),
        out_shape=[jax.ShapeDtypeStruct((2, SHARE, FEATURES), BF16)] * Z_SIZE,
        compiler_params=params(),
        cost_estimate=cost(MIB),
    )(at, blocks)


def z_sum_kernel(*refs):
    early, late, (grad_u, grad_v) = refs[:Z_SIZE], refs[Z_SIZE : 2 * Z_SIZE], refs[2 * Z_SIZE :]

    def total(blocks, which):
        a, b, c, d = (block[which].astype(F32) for block in blocks)
        return (a + b) + (c + d)

    grad_u[0] = total(early, 0)
    grad_v[1] = total(early, 1)
    grad_u[1] = total(late, 0)
    grad_v[0] = total(late, 1)


def z_sum(early, late):
    return pl.pallas_call(
        z_sum_kernel,
        out_shape=[jax.ShapeDtypeStruct((2, SHARE, FEATURES), F32)] * 2,
        compiler_params=params(),
        cost_estimate=cost(2 * MIB),
    )(*early, *late)


def last_kernel(at, back, pooled, proj, grad_pooled, grad_proj, grad_bias):
    step = pl.program_id(0)
    factor = masked_projection(proj, at[AT_WIDTH])
    none = jnp.zeros_like(factor)
    both = jnp.concatenate(
        [jnp.concatenate([factor, none], axis=1), jnp.concatenate([none, factor], axis=1)], axis=0
    )
    total = jnp.zeros((PROJ, EMB), F32)
    bias = jnp.zeros((1, EMB), F32)
    for block in range(back.shape[0]):
        grads = back[block, :HALF, :]
        start = block * SAMPLES
        out = dot(grads, both, 1, 0).astype(BF16)
        grad_pooled[start : start + HALF, :] = out[:, :EMB]
        grad_pooled[start + HALF : start + SAMPLES, :] = out[:, EMB:]
        upper = dot(grads, pooled[start : start + HALF, :], 0, 0)
        lower = dot(grads, pooled[start + HALF : start + SAMPLES, :], 0, 0)
        total += upper[:PROJ] + lower[PROJ:]
        bias += back[block, HALF:, :].astype(F32)[:1]

    bias = jnp.concatenate([bias[:, :PROJ], bias[:, PROJ:]], axis=0)

    @pl.when(step == 0)
    def _():
        grad_proj[...] = total
        grad_bias[...] = bias

    @pl.when(step > 0)
    def _():
        grad_proj[...] += total
        grad_bias[...] += bias


def last(at, back, pooled, proj):
    blocks = 8
    return pl.pallas_call(
        last_kernel,
        grid_spec=pltpu.PrefetchScalarGridSpec(
            num_scalar_prefetch=1,
            grid=(FIELD_TABLES // blocks,),
            in_specs=[
                pl.BlockSpec((blocks, BACK_ROWS, EMB), lambda i, at: (i, 0, 0)),
                pl.BlockSpec((blocks * SAMPLES, EMB), lambda i, at: (i, 0)),
                pl.BlockSpec((1, PROJ, EMB), lambda i, at: (at[AT_BATCH], 0, 0)),
            ],
            out_specs=[
                pl.BlockSpec((blocks * SAMPLES, EMB), lambda i, at: (i, 0)),
                whole_spec(PROJ, EMB),
                whole_spec(2, PROJ),
            ],
        ),
        out_shape=[
            jax.ShapeDtypeStruct((TOKENS, EMB), BF16),
            jax.ShapeDtypeStruct((PROJ, EMB), F32),
            jax.ShapeDtypeStruct((2, PROJ), F32),
        ],
        compiler_params=params(),
        cost_estimate=cost(5 * MIB),
    )(at, back, pooled, proj)


def batch_moves(move):
    pairs = []
    for source in range(X_SIZE * Z_SIZE * CORES):
        x, z, core = source // (Z_SIZE * CORES), source // CORES % Z_SIZE, source % CORES
        x, z, core = move(x, z, core)
        pairs.append((source, (x * Z_SIZE + z) * CORES + core))
    return pairs


def field_moves(move):
    pairs = []
    for source in range(Y_SIZE * HALVES):
        y, half = move(source // HALVES, source % HALVES)
        pairs.append((source, y * HALVES + half))
    return pairs


CORE_SWAP = batch_moves(lambda x, z, core: (x, z, 1 - core))
Z_MOVES = [batch_moves(lambda x, z, core, s=s: (x, (z + s) % Z_SIZE, core)) for s in range(Z_SIZE)]
X_GROUPS = [
    [(x * Z_SIZE + z) * CORES + core for x in range(X_SIZE)] for z in range(Z_SIZE) for core in range(CORES)
]
Y_MOVES = [field_moves(lambda y, half, s=s: ((y + s) % Y_SIZE, half)) for s in range(Y_SIZE)]
HALF_SWAP = field_moves(lambda y, half: (y, 1 - half))


def exchange(parts, axis, moves):
    return [parts[0]] + [lax.ppermute(parts[s], axis, moves[s]) for s in range(1, len(parts))]


def scatter_sum(blocks, groups):
    return lax.psum_scatter(
        blocks, "batch", scatter_dimension=0, tiled=True, axis_index_groups=groups
    )


def low_sum(parts):
    wide = [part.astype(F32) for part in parts]
    total = wide[0]
    for part in wide[1:]:
        total = total + part
    return total.astype(BF16)


def to_all(blocks):
    return lax.all_to_all(blocks, "batch", split_axis=0, concat_axis=0, tiled=True)


def in_hbm(value):
    return pltpu.with_memory_space_constraint(value, pltpu.HBM)


def after(value, earlier):
    return lax.optimization_barrier((value, earlier))[0]


def core_swap(value):
    return lax.ppermute(value, "batch", CORE_SWAP)


def both_halves(partial):
    return low_sum([partial, lax.ppermute(partial, "field", HALF_SWAP)])


def on_device(
    emb_tables, bag_ids, bag_lengths, table_widths, projection, cross_u, cross_v, cross_bias, cotangent
):
    batch = lax.axis_index("batch")
    field = lax.axis_index("field")
    at = jnp.stack(
        [batch, batch // (Z_SIZE * CORES), batch // CORES % Z_SIZE, batch % CORES, field // HALVES, table_widths[0]]
    ).astype(jnp.int32)
    shard = jnp.concatenate([cross_u, cross_v], axis=0)
    weights = lax.all_gather(shard, "batch", axis=0, tiled=True)
    weights = in_hbm(weights.reshape(FIELD_TABLES, 4, SHARE, FEATURES))
    proj = jnp.transpose(projection, (0, 2, 1))

    places = lax.broadcasted_iota(jnp.int32, (BAG, TOKENS), 0)
    ids = jnp.where(places < bag_lengths, bag_ids[0].T, ROWS)
    ids = ids.reshape(BAG, TOKENS // 128, 128).transpose(1, 0, 2).reshape(-1)
    pooled, sent = pool(at, ids, in_hbm(emb_tables[0]), proj)
    recv = to_all(sent)

    pair_0, sum1 = unpack(recv, cotangent)
    parts = first(at, pair_0, weights)
    other_0 = core_swap(pair_0)
    parts = exchange(parts, "field", Y_MOVES)
    partial = low_sum([after(parts[0], other_0)] + parts[1:])
    ranks = assemble(at, exchange([both_halves(partial)] * Y_SIZE, "field", Y_MOVES))
    other_ranks = core_swap(ranks)

    pair_1, base, sum0, *parts = second(at, ranks, pair_0, cotangent, weights, cross_bias)
    blocks = terms(at, ranks, other_ranks, pair_1, core_swap(pair_1))
    early = scatter_sum(blocks, X_GROUPS)[0]
    parts = exchange(parts, "field", Y_MOVES)
    partial = low_sum([after(parts[0], blocks)] + parts[1:])
    ranks = assemble(at, exchange([both_halves(partial)] * Y_SIZE, "field", Y_MOVES))

    blocks = terms(at, ranks, core_swap(ranks), pair_0, other_0)
    crossed, back = third(
        at,
        after(ranks, blocks),
        in_hbm(pair_0),
        in_hbm(pair_1),
        in_hbm(cotangent),
        in_hbm(base),
        weights,
        cross_bias,
        sum0,
        sum1,
    )
    early = exchange(z_split(at, early), "batch", Z_MOVES)
    returned = to_all(after(back, early[1:]))
    late = exchange(z_split(at, scatter_sum(blocks, X_GROUPS)[0]), "batch", Z_MOVES)
    returned = after(returned, late[0])
    grad_pooled, grad_proj, grad_bias = last(at, returned, in_hbm(pooled), proj)
    grad_u, grad_v = z_sum(early, [after(late[0], grad_proj)] + late[1:])
    return (
        crossed,
        grad_u,
        grad_v,
        grad_bias,
        grad_proj.T[None],
        grad_pooled[None],
    )


def solution(mesh):
    return jax.shard_map(
        on_device,
        mesh=mesh,
        in_specs=(
            P(("field", "batch"), None, None),
            P(("field", "batch"), None, None),
            P(("field", "batch"), None),
            P(("field", "batch")),
            P("field", None, None),
            P(None, "batch", "field"),
            P(None, "batch", "field"),
            P(None, "field"),
            P("batch", "field"),
        ),
        out_specs=(
            P("batch", "field"),
            P(None, "batch", "field"),
            P(None, "batch", "field"),
            P(None, ("field", "batch")),
            P(("field", "batch"), None, None),
            P(("field", "batch"), None, None),
        ),
        check_vma=False,
    )
```

```python
import functools

import jax
import jax.numpy as jnp
from jax import lax
from jax.experimental import pallas as pl
from jax.experimental.pallas import tpu as pltpu
from jax.sharding import PartitionSpec as P

BF16 = jnp.bfloat16
F32 = jnp.float32
MIB = 2**20

X_SIZE, Z_SIZE, CORES = 4, 4, 2
Y_SIZE, HALVES = 4, 2

ROWS, EMB, PROJ, BAG = 8192, 128, 64, 8
SAMPLES, FEATURES, RANK = 192, 2048, 512
FIELD_TABLES = 32
HALF = SAMPLES // 2
SHARE = RANK // FIELD_TABLES
TOKENS = SAMPLES * FIELD_TABLES
BACK_ROWS = HALF + 16
FEATURE_BLOCK = 1024
POOL_CHUNK = 1536
POOL_UNROLL = 64
QUARTER = 2 * SAMPLES // Y_SIZE

AT_BATCH, AT_X, AT_Z, AT_CORE, AT_Y, AT_WIDTH = range(6)
U0, U1, V0, V1 = range(4)


def params():
    return pltpu.CompilerParams(vmem_limit_bytes=32 * MIB)


def cost(moved):
    return pl.CostEstimate(flops=0, bytes_accessed=moved, transcendentals=0)


def dot(left, right, left_dim, right_dim):
    return lax.dot_general(
        left, right, (((left_dim,), (right_dim,)), ((), ())), preferred_element_type=F32
    )


def masked_projection(proj_ref, width):
    columns = lax.broadcasted_iota(jnp.int32, (PROJ, EMB), 1)
    return jnp.where(columns < width, proj_ref[0].astype(F32), 0.0).astype(BF16)


def pool_kernel(at, ids, table, proj, pooled, sent, wide_table, summed):
    @pl.when(pl.program_id(0) == 0)
    def _():
        within = lax.broadcasted_iota(jnp.int32, (256, EMB), 1) < at[AT_WIDTH]

        @pl.loop(0, ROWS // 256)
        def _(part):
            rows = pl.ds(pl.multiple_of(part * 256, 256), 256)
            wide_table[rows, :] = jnp.where(within, table[rows, :].astype(F32), 0.0)

        wide_table[ROWS : ROWS + 8, :] = jnp.zeros((8, EMB), F32)

    groups = 128 // POOL_UNROLL

    @pl.loop(0, POOL_CHUNK // POOL_UNROLL)
    def _(group):
        first = group * POOL_UNROLL
        base = (group // groups) * (128 * BAG) + (group % groups) * POOL_UNROLL
        for step in range(POOL_UNROLL):
            rows = [wide_table[pl.ds(ids[base + (place * 128 + step)], 1), :] for place in range(BAG)]
            summed[pl.ds(first + step, 1), :] = (
                (rows[0] + rows[1]) + (rows[2] + rows[3])
            ) + ((rows[4] + rows[5]) + (rows[6] + rows[7]))

    low = summed[...].astype(BF16)
    pooled[...] = low
    factor = proj[0]
    none = jnp.zeros_like(factor)
    both = jnp.concatenate(
        [jnp.concatenate([factor, none], axis=1), jnp.concatenate([none, factor], axis=1)], axis=0
    )
    for block in range(POOL_CHUNK // SAMPLES):
        start = block * SAMPLES
        pair = jnp.concatenate(
            [low[start : start + HALF], low[start + HALF : start + SAMPLES]], axis=1
        )
        sent[block] = dot(pair, both, 1, 1).astype(BF16)


def pool(at, ids, table, proj):
    blocks = POOL_CHUNK // SAMPLES
    return pl.pallas_call(
        pool_kernel,
        grid_spec=pltpu.PrefetchScalarGridSpec(
            num_scalar_prefetch=1,
            grid=(TOKENS // POOL_CHUNK,),
            in_specs=[
                pl.BlockSpec((POOL_CHUNK * BAG,), lambda i, at: (i,), memory_space=pltpu.SMEM),
                pl.BlockSpec((ROWS, EMB), lambda i, at: (0, 0)),
                pl.BlockSpec((1, PROJ, EMB), lambda i, at: (at[AT_BATCH], 0, 0)),
            ],
            out_specs=[
                pl.BlockSpec((POOL_CHUNK, EMB), lambda i, at: (i, 0)),
                pl.BlockSpec((blocks, HALF, EMB), lambda i, at: (i, 0, 0)),
            ],
            scratch_shapes=[pltpu.VMEM((ROWS + 8, EMB), F32), pltpu.VMEM((POOL_CHUNK, EMB), F32)],
        ),
        out_shape=[
            jax.ShapeDtypeStruct((TOKENS, EMB), BF16),
            jax.ShapeDtypeStruct((FIELD_TABLES, HALF, EMB), BF16),
        ],
        compiler_params=params(),
        cost_estimate=cost(100 * MIB),
    )(at, ids, table, proj)


def assemble_kernel(at, *refs):
    parts, whole = refs[:-1], refs[-1]
    for shift, part in enumerate(parts):
        place = lax.rem(at[AT_Y] + Y_SIZE - shift, Y_SIZE)
        whole[pl.ds(pl.multiple_of(place * QUARTER, QUARTER), QUARTER), :] = part[...]


def assemble(at, parts):
    return pl.pallas_call(
        assemble_kernel,
        grid_spec=pltpu.PrefetchScalarGridSpec(
            num_scalar_prefetch=1,
            grid=(1,),
            in_specs=[whole_spec(QUARTER, RANK)] * Y_SIZE,
            out_specs=whole_spec(2 * SAMPLES, RANK),
        ),
        out_shape=jax.ShapeDtypeStruct((2 * SAMPLES, RANK), BF16),
        compiler_params=params(),
        cost_estimate=cost(MIB),
    )(at, *parts)


def write_quarters(at, total, parts):
    for shift, part in enumerate(parts):
        place = lax.rem(at[AT_Y] + shift, Y_SIZE)
        part[...] = total[pl.ds(pl.multiple_of(place * QUARTER, QUARTER), QUARTER), :].astype(BF16)


def weight(ref):
    return ref[...].reshape(RANK, FEATURE_BLOCK)


def unpack_kernel(recv, cot, pair, bias_out):
    columns = []
    for place in range(FEATURE_BLOCK // EMB):
        left, right = recv[2 * place], recv[2 * place + 1]
        top = jnp.concatenate([left[:, :PROJ], right[:, :PROJ]], axis=1)
        bottom = jnp.concatenate([left[:, PROJ:], right[:, PROJ:]], axis=1)
        columns.append(jnp.concatenate([top, bottom], axis=0))
    x0 = jnp.concatenate(columns, axis=1)
    hg = (cot[...].astype(F32) * x0.astype(F32)).astype(BF16)
    pair[0] = hg
    pair[1] = x0
    bias_out[...] = jnp.sum(hg.astype(F32), axis=0, keepdims=True)


def unpack(recv, cot):
    return pl.pallas_call(
        unpack_kernel,
        grid=(FEATURE_STEPS,),
        in_specs=[
            pl.BlockSpec((TABLES_STEP, HALF, EMB), lambda j: (j, 0, 0)),
            pl.BlockSpec((SAMPLES, FEATURE_BLOCK), lambda j: (0, j)),
        ],
        out_specs=[
            pl.BlockSpec((2, SAMPLES, FEATURE_BLOCK), lambda j: (0, 0, j)),
            pl.BlockSpec((1, FEATURE_BLOCK), lambda j: (0, j)),
        ],
        out_shape=[
            jax.ShapeDtypeStruct((2, SAMPLES, FEATURES), BF16),
            jax.ShapeDtypeStruct((1, FEATURES), F32),
        ],
        compiler_params=params(),
        cost_estimate=cost(4 * MIB),
    )(recv, cot)


def first_kernel(at, pair, v0, u1, q0, q1, q2, q3, total):
    step = pl.program_id(0)
    rank = dot(pair[1], weight(v0), 1, 1)
    rank_grad = dot(pair[0], weight(u1), 1, 1)

    @pl.when(step == 0)
    def _():
        total[:SAMPLES, :] = rank
        total[SAMPLES:, :] = rank_grad

    @pl.when(step > 0)
    def _():
        total[:SAMPLES, :] += rank
        total[SAMPLES:, :] += rank_grad

    @pl.when(step == pl.num_programs(0) - 1)
    def _():
        write_quarters(at, total, (q0, q1, q2, q3))


def feature_spec(rows):
    return pl.BlockSpec((rows, FEATURE_BLOCK), lambda j, at: (0, j))


def weight_spec(which):
    return pl.BlockSpec(
        (FIELD_TABLES, 1, SHARE, FEATURE_BLOCK), lambda j, at: (0, which, 0, j)
    )


def whole_spec(*shape):
    return pl.BlockSpec(shape, lambda j, at: (0,) * len(shape))


def pair_spec(which=None):
    if which is None:
        return pl.BlockSpec((2, SAMPLES, FEATURE_BLOCK), lambda j, at: (0, 0, j))
    return pl.BlockSpec((None, SAMPLES, FEATURE_BLOCK), lambda j, at: (which, 0, j))


QUARTER_SPECS = [whole_spec(QUARTER, RANK)] * Y_SIZE
QUARTER_SHAPES = [jax.ShapeDtypeStruct((QUARTER, RANK), BF16)] * Y_SIZE
FEATURE_STEPS = FEATURES // FEATURE_BLOCK
TABLES_STEP = FEATURE_BLOCK // PROJ


def first(at, pair, weights):
    return pl.pallas_call(
        first_kernel,
        grid_spec=pltpu.PrefetchScalarGridSpec(
            num_scalar_prefetch=1,
            grid=(FEATURE_STEPS,),
            in_specs=[pair_spec(), weight_spec(V0), weight_spec(U1)],
            out_specs=QUARTER_SPECS,
            scratch_shapes=[pltpu.VMEM((2 * SAMPLES, RANK), F32)],
        ),
        out_shape=QUARTER_SHAPES,
        compiler_params=params(),
        cost_estimate=cost(8 * MIB),
    )(at, pair, weights, weights)


def second_kernel(at, ranks, x0_ref, cot, u0_ref, v1_ref, bias, pair, base_out, bias_out, q0, q1, q2, q3, total):
    step = pl.program_id(0)
    u0, v1 = weight(u0_ref), weight(v1_ref)
    x0 = x0_ref[...].astype(F32)
    hidden = dot(ranks[:SAMPLES, :], u0, 1, 0) + bias[0:1, :]
    upstream = cot[...].astype(F32) + dot(ranks[SAMPLES:, :], v1, 1, 0)
    x1 = (x0 * hidden + x0).astype(BF16)
    hg = (upstream * x0).astype(BF16)
    pair[0] = hg
    pair[1] = x1
    base_out[...] = upstream + upstream * hidden
    bias_out[...] = jnp.sum(hg.astype(F32), axis=0, keepdims=True)
    rank = dot(x1, v1, 1, 1)
    rank_grad = dot(hg, u0, 1, 1)

    @pl.when(step == 0)
    def _():
        total[:SAMPLES, :] = rank
        total[SAMPLES:, :] = rank_grad

    @pl.when(step > 0)
    def _():
        total[:SAMPLES, :] += rank
        total[SAMPLES:, :] += rank_grad

    @pl.when(step == pl.num_programs(0) - 1)
    def _():
        write_quarters(at, total, (q0, q1, q2, q3))


def second(at, ranks, pair, cot, weights, bias):
    return pl.pallas_call(
        second_kernel,
        grid_spec=pltpu.PrefetchScalarGridSpec(
            num_scalar_prefetch=1,
            grid=(FEATURE_STEPS,),
            in_specs=[
                whole_spec(2 * SAMPLES, RANK),
                pair_spec(1),
                feature_spec(SAMPLES),
                weight_spec(U0),
                weight_spec(V1),
                feature_spec(2),
            ],
            out_specs=[
                pair_spec(),
                feature_spec(SAMPLES),
                feature_spec(1),
            ]
            + QUARTER_SPECS,
            scratch_shapes=[pltpu.VMEM((2 * SAMPLES, RANK), F32)],
        ),
        out_shape=[
            jax.ShapeDtypeStruct((2, SAMPLES, FEATURES), BF16),
            jax.ShapeDtypeStruct((SAMPLES, FEATURES), F32),
            jax.ShapeDtypeStruct((1, FEATURES), F32),
        ]
        + QUARTER_SHAPES,
        compiler_params=params(),
        cost_estimate=cost(10 * MIB),
    )(at, ranks, pair, cot, weights, weights, bias)


def third_kernel(at, ranks, x0_ref, x1_ref, cot, base, u1_ref, v0_ref, bias, sum0, sum1, crossed, back):
    hidden = dot(ranks[:SAMPLES, :], weight(u1_ref), 1, 0) + bias[1:2, :]
    crossed[...] = (x0_ref[...].astype(F32) * hidden + x1_ref[...].astype(F32)).astype(BF16)
    grad = base[...] + dot(ranks[SAMPLES:, :], weight(v0_ref), 1, 0) + cot[...].astype(F32) * hidden
    grad = grad.astype(BF16)
    for table in range(TABLES_STEP):
        columns = slice(table * PROJ, (table + 1) * PROJ)
        back[table, :HALF, :] = jnp.concatenate([grad[:HALF, columns], grad[HALF:, columns]], axis=1)
        row = jnp.concatenate([sum0[:, columns], sum1[:, columns]], axis=1)
        first_row = lax.broadcasted_iota(jnp.int32, (16, EMB), 0) == 0
        back[table, HALF:, :] = jnp.where(first_row, row, 0.0).astype(BF16)


def third(at, ranks, pair_0, pair_1, cot, base, weights, bias, sum0, sum1):
    return pl.pallas_call(
        third_kernel,
        grid_spec=pltpu.PrefetchScalarGridSpec(
            num_scalar_prefetch=1,
            grid=(FEATURE_STEPS,),
            in_specs=[whole_spec(2 * SAMPLES, RANK), pair_spec(1), pair_spec(1)]
            + [feature_spec(SAMPLES)] * 2
            + [weight_spec(U1), weight_spec(V0), feature_spec(2), feature_spec(1), feature_spec(1)],
            out_specs=[
                feature_spec(SAMPLES),
                pl.BlockSpec((TABLES_STEP, BACK_ROWS, EMB), lambda j, at: (j, 0, 0)),
            ],
        ),
        out_shape=[
            jax.ShapeDtypeStruct((SAMPLES, FEATURES), BF16),
            jax.ShapeDtypeStruct((FIELD_TABLES, BACK_ROWS, EMB), BF16),
        ],
        compiler_params=params(),
        cost_estimate=cost(MIB),
    )(at, ranks, pair_0, pair_1, cot, base, weights, weights, bias, sum0, sum1)


def terms_kernel(at, ranks, other_ranks, pair, other_pair, out, sides):
    @pl.when(pl.program_id(0) == 0)
    def _():
        is_first = at[AT_CORE] == 0
        for which in range(2):
            part = slice(which * SAMPLES, (which + 1) * SAMPLES)
            rows = jnp.concatenate([ranks[part, :], other_ranks[part, :]], axis=0).astype(F32)
            turned = rows.T.reshape(RANK // (CORES * SHARE), CORES, SHARE, 2 * SAMPLES)
            mine = jnp.where(is_first, turned[:, 0], turned[:, 1])
            sides[which] = mine.reshape(RANK // CORES, 2 * SAMPLES).astype(BF16)

    for which in range(2):
        side = jnp.concatenate([pair[which], other_pair[which]], axis=0)
        term = dot(sides[which], side, 1, 0).astype(BF16)
        out[:, :, which] = term.reshape(X_SIZE, Z_SIZE, SHARE, FEATURE_BLOCK)


GRAD_SHAPE = (X_SIZE, Z_SIZE, 2, SHARE, FEATURES)


def terms(at, ranks, other_ranks, pair, other_pair):
    return pl.pallas_call(
        terms_kernel,
        grid_spec=pltpu.PrefetchScalarGridSpec(
            num_scalar_prefetch=1,
            grid=(FEATURE_STEPS,),
            in_specs=[whole_spec(2 * SAMPLES, RANK)] * 2 + [pair_spec()] * 2,
            out_specs=pl.BlockSpec(GRAD_SHAPE[:-1] + (FEATURE_BLOCK,), lambda j, at: (0, 0, 0, 0, j)),
            scratch_shapes=[pltpu.VMEM((2, RANK // CORES, 2 * SAMPLES), BF16)],
        ),
        out_shape=jax.ShapeDtypeStruct(GRAD_SHAPE, BF16),
        compiler_params=params(),
        cost_estimate=cost(6 * MIB),
    )(at, ranks, other_ranks, pair, other_pair)


def z_split_kernel(at, blocks, *outs):
    for shift, out in enumerate(outs):
        out[...] = blocks[lax.rem(at[AT_Z] + shift, Z_SIZE)]


def z_split(at, blocks):
    return pl.pallas_call(
        z_split_kernel,
        grid_spec=pltpu.PrefetchScalarGridSpec(
            num_scalar_prefetch=1,
            grid=(1,),
            in_specs=[whole_spec(*GRAD_SHAPE[1:])],
            out_specs=[whole_spec(2, SHARE, FEATURES)] * Z_SIZE,
        ),
        out_shape=[jax.ShapeDtypeStruct((2, SHARE, FEATURES), BF16)] * Z_SIZE,
        compiler_params=params(),
        cost_estimate=cost(MIB),
    )(at, blocks)


def z_sum_kernel(*refs):
    early, late, (grad_u, grad_v) = refs[:Z_SIZE], refs[Z_SIZE : 2 * Z_SIZE], refs[2 * Z_SIZE :]

    def total(blocks, which):
        a, b, c, d = (block[which].astype(F32) for block in blocks)
        return (a + b) + (c + d)

    grad_u[0] = total(early, 0)
    grad_v[1] = total(early, 1)
    grad_u[1] = total(late, 0)
    grad_v[0] = total(late, 1)


def z_sum(early, late):
    return pl.pallas_call(
        z_sum_kernel,
        out_shape=[jax.ShapeDtypeStruct((2, SHARE, FEATURES), F32)] * 2,
        compiler_params=params(),
        cost_estimate=cost(2 * MIB),
    )(*early, *late)


def last_kernel(at, back, pooled, proj, grad_pooled, grad_proj, grad_bias):
    step = pl.program_id(0)
    factor = masked_projection(proj, at[AT_WIDTH])
    none = jnp.zeros_like(factor)
    both = jnp.concatenate(
        [jnp.concatenate([factor, none], axis=1), jnp.concatenate([none, factor], axis=1)], axis=0
    )
    blocks = back.shape[0]
    grads = back[:, :HALF, :].reshape(blocks * HALF, EMB)
    out = dot(grads, both, 1, 0).astype(BF16)
    halves = [out[:, :EMB].reshape(blocks, HALF, EMB), out[:, EMB:].reshape(blocks, HALF, EMB)]
    grad_pooled[...] = jnp.concatenate(halves, axis=1).reshape(blocks * SAMPLES, EMB)
    bags = pooled[...].reshape(blocks, SAMPLES, EMB)
    upper = bags[:, :HALF].reshape(blocks * HALF, EMB)
    lower = bags[:, HALF:].reshape(blocks * HALF, EMB)
    products = dot(grads, jnp.concatenate([upper, lower], axis=1), 0, 0)
    total = products[:PROJ, :EMB] + products[PROJ:, EMB:]
    bias = jnp.sum(back[:, HALF:, :].astype(F32), axis=0)[:1]
    bias = jnp.concatenate([bias[:, :PROJ], bias[:, PROJ:]], axis=0)

    @pl.when(step == 0)
    def _():
        grad_proj[...] = total
        grad_bias[...] = bias

    @pl.when(step > 0)
    def _():
        grad_proj[...] += total
        grad_bias[...] += bias


def last(at, back, pooled, proj):
    blocks = 8
    return pl.pallas_call(
        last_kernel,
        grid_spec=pltpu.PrefetchScalarGridSpec(
            num_scalar_prefetch=1,
            grid=(FIELD_TABLES // blocks,),
            in_specs=[
                pl.BlockSpec((blocks, BACK_ROWS, EMB), lambda i, at: (i, 0, 0)),
                pl.BlockSpec((blocks * SAMPLES, EMB), lambda i, at: (i, 0)),
                pl.BlockSpec((1, PROJ, EMB), lambda i, at: (at[AT_BATCH], 0, 0)),
            ],
            out_specs=[
                pl.BlockSpec((blocks * SAMPLES, EMB), lambda i, at: (i, 0)),
                whole_spec(PROJ, EMB),
                whole_spec(2, PROJ),
            ],
        ),
        out_shape=[
            jax.ShapeDtypeStruct((TOKENS, EMB), BF16),
            jax.ShapeDtypeStruct((PROJ, EMB), F32),
            jax.ShapeDtypeStruct((2, PROJ), F32),
        ],
        compiler_params=params(),
        cost_estimate=cost(5 * MIB),
    )(at, back, pooled, proj)


def batch_moves(move):
    pairs = []
    for source in range(X_SIZE * Z_SIZE * CORES):
        x, z, core = source // (Z_SIZE * CORES), source // CORES % Z_SIZE, source % CORES
        x, z, core = move(x, z, core)
        pairs.append((source, (x * Z_SIZE + z) * CORES + core))
    return pairs


def field_moves(move):
    pairs = []
    for source in range(Y_SIZE * HALVES):
        y, half = move(source // HALVES, source % HALVES)
        pairs.append((source, y * HALVES + half))
    return pairs


CORE_SWAP = batch_moves(lambda x, z, core: (x, z, 1 - core))
Z_MOVES = [batch_moves(lambda x, z, core, s=s: (x, (z + s) % Z_SIZE, core)) for s in range(Z_SIZE)]
X_GROUPS = [
    [(x * Z_SIZE + z) * CORES + core for x in range(X_SIZE)] for z in range(Z_SIZE) for core in range(CORES)
]
Y_MOVES = [field_moves(lambda y, half, s=s: ((y + s) % Y_SIZE, half)) for s in range(Y_SIZE)]
HALF_SWAP = field_moves(lambda y, half: (y, 1 - half))


def exchange(parts, axis, moves):
    return [parts[0]] + [lax.ppermute(parts[s], axis, moves[s]) for s in range(1, len(parts))]


def scatter_sum(blocks, groups):
    return lax.psum_scatter(
        blocks, "batch", scatter_dimension=0, tiled=True, axis_index_groups=groups
    )


def low_sum(parts):
    wide = [part.astype(F32) for part in parts]
    total = wide[0]
    for part in wide[1:]:
        total = total + part
    return total.astype(BF16)


def to_all(blocks):
    return lax.all_to_all(blocks, "batch", split_axis=0, concat_axis=0, tiled=True)


def in_hbm(value):
    return pltpu.with_memory_space_constraint(value, pltpu.HBM)


def after(value, earlier):
    return lax.optimization_barrier((value, earlier))[0]


def core_swap(value):
    return lax.ppermute(value, "batch", CORE_SWAP)


def both_halves(partial):
    return low_sum([partial, lax.ppermute(partial, "field", HALF_SWAP)])


def on_device(
    emb_tables, bag_ids, bag_lengths, table_widths, projection, cross_u, cross_v, cross_bias, cotangent
):
    batch = lax.axis_index("batch")
    field = lax.axis_index("field")
    at = jnp.stack(
        [batch, batch // (Z_SIZE * CORES), batch // CORES % Z_SIZE, batch % CORES, field // HALVES, table_widths[0]]
    ).astype(jnp.int32)
    shard = jnp.concatenate([cross_u, cross_v], axis=0)
    weights = lax.all_gather(shard, "batch", axis=0, tiled=True)
    weights = in_hbm(weights.reshape(FIELD_TABLES, 4, SHARE, FEATURES))
    proj = jnp.transpose(projection, (0, 2, 1))

    places = lax.broadcasted_iota(jnp.int32, (BAG, TOKENS), 0)
    ids = jnp.where(places < bag_lengths, bag_ids[0].T, ROWS)
    ids = ids.reshape(BAG, TOKENS // 128, 128).transpose(1, 0, 2).reshape(-1)
    pooled, sent = pool(at, ids, in_hbm(emb_tables[0]), proj)
    recv = to_all(sent)

    pair_0, sum1 = unpack(recv, cotangent)
    parts = first(at, pair_0, weights)
    other_0 = core_swap(pair_0)
    parts = exchange(parts, "field", Y_MOVES)
    partial = low_sum([after(parts[0], other_0)] + parts[1:])
    ranks = assemble(at, exchange([both_halves(partial)] * Y_SIZE, "field", Y_MOVES))
    other_ranks = core_swap(ranks)

    pair_1, base, sum0, *parts = second(at, ranks, pair_0, cotangent, weights, cross_bias)
    blocks = terms(at, ranks, other_ranks, pair_1, core_swap(pair_1))
    early = scatter_sum(blocks, X_GROUPS)[0]
    parts = exchange(parts, "field", Y_MOVES)
    partial = low_sum([after(parts[0], blocks)] + parts[1:])
    ranks = assemble(at, exchange([both_halves(partial)] * Y_SIZE, "field", Y_MOVES))

    blocks = terms(at, ranks, core_swap(ranks), pair_0, other_0)
    crossed, back = third(
        at,
        after(ranks, blocks),
        in_hbm(pair_0),
        in_hbm(pair_1),
        in_hbm(cotangent),
        in_hbm(base),
        weights,
        cross_bias,
        sum0,
        sum1,
    )
    early = exchange(z_split(at, early), "batch", Z_MOVES)
    returned = to_all(after(back, early[1:]))
    late = exchange(z_split(at, scatter_sum(blocks, X_GROUPS)[0]), "batch", Z_MOVES)
    returned = after(returned, late[0])
    grad_pooled, grad_proj, grad_bias = last(at, returned, in_hbm(pooled), proj)
    grad_u, grad_v = z_sum(early, [after(late[0], grad_proj)] + late[1:])
    return (
        crossed,
        grad_u,
        grad_v,
        grad_bias,
        grad_proj.T[None],
        grad_pooled[None],
    )


def solution(mesh):
    return jax.shard_map(
        on_device,
        mesh=mesh,
        in_specs=(
            P(("field", "batch"), None, None),
            P(("field", "batch"), None, None),
            P(("field", "batch"), None),
            P(("field", "batch")),
            P("field", None, None),
            P(None, "batch", "field"),
            P(None, "batch", "field"),
            P(None, "field"),
            P("batch", "field"),
        ),
        out_specs=(
            P("batch", "field"),
            P(None, "batch", "field"),
            P(None, "batch", "field"),
            P(None, ("field", "batch")),
            P(("field", "batch"), None, None),
            P(("field", "batch"), None, None),
        ),
        check_vma=False,
    )
```
